512 devices in a mesh: ch: 512 (over z, y, x, core).
Axes of the slice: x: 4, y: 8, z: 8, core: 2. Of those that a mesh axis runs over, the one named last changes fastest.
Arguments:
- raw: bfloat16 [4096, 65536], P(None, 'ch')
- taps: float32 [16], replicated, may hold values from -1.2 to 1.2
- offsets: int32 [16], replicated, may hold values from 1 to 256, as said below
- sources: int32 [32], replicated, may hold values from 0 to 65535, as said below
- edges: int32 [17], replicated, may hold values from 0 to 128, as said below
Outputs:
- coherence: float32 [16, 32, 65536], P(None, None, 'ch')
- correlation: float32 [32, 129, 65536], P(None, None, 'ch')
The draws below stay inside these ranges and needn't reach their ends.
Inputs may be any that keep to these rules, and one draw needn't show every extreme that they name: offsets may repeat. `sources`: distinct channels. edges rise; edges[0] = 0, edges[16] = 128, each band holds at least 4 bins.
All inputs are finite; a program needn't handle non-finite values.
Results may differ from the reference program's by a relative error of at most 0.004.
Values may be sent and summed in bfloat16 or wider, within the bound.
No kernel may reach another device: no remote copies, remote signals or barrier semaphores. Data moves between devices by JAX's collectives and lax.ppermute only.
A program may use at most 128 MiB of HBM per device.

```python
import math
import jax
import jax.numpy as jnp
from jax import lax

CH_DEV = 128
SAMPLES = 4096
DEC = 2
TAPS = 16
NFFT = 256
BANDS = 16
SOURCES = 32
OFFS = 16
MAXLAG = 64
NCH = 65536
DECIM = 2048
FRAMES = 8
NBIN = 128
REACH = 256
LAGS = 129
N_CH = 512


def draw_raw(key, part):
    key_base, key_scale = jax.random.split(key, 2)
    blocks = SAMPLES // (DEC * NFFT)
    base = jax.random.normal(key_base, (SAMPLES, NCH), jnp.float32)
    scales = jnp.exp(jax.random.uniform(key_scale, (blocks, NCH), jnp.float32, 0.0, math.log(10.0)))
    return (jnp.repeat(scales, DEC * NFFT, axis=0) * base).astype(jnp.bfloat16)


def draw_offsets(key, part):
    key_vals, key_order = jax.random.split(jax.random.fold_in(key, 11))
    middle = jax.random.randint(key_vals, (OFFS - 2,), 1, REACH + 1).astype(jnp.int32)
    values = jnp.concatenate([jnp.array([1, REACH], jnp.int32), middle])
    return values[jax.random.permutation(key_order, OFFS)]


def draw_sources(key, part):
    key_vals, key_order = jax.random.split(jax.random.fold_in(key, 23))
    inner = (jax.random.permutation(key_vals, NCH - 2)[:SOURCES - 2] + 1).astype(jnp.int32)
    values = jnp.concatenate([jnp.array([0, NCH - 1], jnp.int32), inner])
    return values[jax.random.permutation(key_order, SOURCES)]


def draw_edges(key, part):
    extra = NBIN - 4 * BANDS
    places = extra + BANDS - 1
    cuts = jnp.sort(jax.random.permutation(jax.random.fold_in(key, 37), places)[:BANDS - 1]).astype(jnp.int32)
    bounds = jnp.concatenate([jnp.array([-1], jnp.int32), cuts, jnp.array([places], jnp.int32)])
    widths = 4 + (bounds[1:] - bounds[:-1] - 1)
    return jnp.concatenate([jnp.zeros((1,), jnp.int32), jnp.cumsum(widths).astype(jnp.int32)])


def scatter_about(stream_key, dims, spread, reach, kind=jnp.bfloat16):
    values = spread * jax.random.normal(stream_key, dims, jnp.float32)
    return jnp.clip(values, min=-reach, max=reach).astype(kind)


def setup_inputs(seed: int = 0) -> dict:
    key_list = jax.random.split(jax.random.key(seed), 6)
    raw = draw_raw(jax.random.fold_in(key_list[5], 71), 0)
    taps = scatter_about(key_list[1], (TAPS,), 0.3, 1.2, jnp.float32)
    offsets = draw_offsets(jax.random.fold_in(key_list[5], 71), 0)
    sources = draw_sources(jax.random.fold_in(key_list[5], 71), 0)
    edges = draw_edges(jax.random.fold_in(key_list[5], 71), 0)
    return dict(raw=raw, taps=taps, offsets=offsets, sources=sources, edges=edges)


def decimate(samples, taps):
    padded = jnp.pad(samples.astype(jnp.float32), ((TAPS - 1, 0), (0, 0)))
    total = jnp.zeros((DECIM, samples.shape[1]), jnp.float32)
    for j in range(TAPS):
        start = TAPS - 1 - j
        total = total + taps[j] * padded[start:start + SAMPLES:DEC][:DECIM]
    return total

def dft_table():
    index = jnp.arange(NFFT, dtype=jnp.int32)
    bins = jnp.arange(NBIN, dtype=jnp.int32)
    phase = (bins[:, None] * index[None, :] % NFFT).astype(jnp.float32) * (2.0 * math.pi / NFFT)
    return jnp.concatenate([jnp.cos(phase), -jnp.sin(phase)], axis=0)

def lag_table():
    lagvals = jnp.arange(LAGS, dtype=jnp.int32) - MAXLAG
    bins = jnp.arange(NBIN, dtype=jnp.int32)
    phase = (lagvals[:, None] * bins[None, :] % NFFT).astype(jnp.float32) * (2.0 * math.pi / NFFT)
    return jnp.concatenate([jnp.cos(phase), -jnp.sin(phase)], axis=1)

def band_mask(edges):
    bins = jnp.arange(NBIN, dtype=jnp.int32)
    return ((bins[None, :] >= edges[:-1, None]) & (bins[None, :] < edges[1:, None])).astype(jnp.float32)

def whiten(samples, taps, edges):
    decimated = decimate(samples, taps)
    frames = decimated.reshape(FRAMES, NFFT, samples.shape[1])
    spectrum = jnp.einsum('kn,fnc->fkc', dft_table(), frames, precision=lax.Precision.HIGHEST)
    squares = lax.optimization_barrier(jnp.sum(spectrum[:, :NBIN] ** 2 + spectrum[:, NBIN:] ** 2, axis=0))
    mask = band_mask(edges)
    counts = lax.optimization_barrier(jnp.sum(mask, axis=1))
    power = jnp.dot(mask, squares, precision=lax.Precision.HIGHEST) / (2.0 * FRAMES * counts)[:, None]
    level = jnp.sqrt(power + 1e-06)
    per_bin = jnp.dot(mask.T, level, precision=lax.Precision.HIGHEST)
    per_bin = jnp.concatenate([per_bin, per_bin], axis=0)
    return (spectrum / per_bin[None]).astype(jnp.bfloat16)

def band_cross(white, partner, mask, band_scale):
    w_re = white[:, :NBIN].astype(jnp.float32)
    w_im = white[:, NBIN:].astype(jnp.float32)
    p_re = partner[:, :NBIN].astype(jnp.float32)
    p_im = partner[:, NBIN:].astype(jnp.float32)
    cross_re = lax.optimization_barrier(jnp.sum(w_re * p_re + w_im * p_im, axis=0))
    cross_im = lax.optimization_barrier(jnp.sum(w_im * p_re - w_re * p_im, axis=0))
    band_re = jnp.dot(mask, cross_re, precision=lax.Precision.HIGHEST) * band_scale[:, None]
    band_im = jnp.dot(mask, cross_im, precision=lax.Precision.HIGHEST) * band_scale[:, None]
    return jnp.concatenate([band_re, band_im], axis=0)

def correlate(source_white, white):
    s_re = source_white[:, :NBIN].astype(jnp.float32)
    s_im = source_white[:, NBIN:].astype(jnp.float32)
    right = jnp.concatenate([white[:, :NBIN], white[:, NBIN:]], axis=0).astype(jnp.float32)
    left_re = jnp.concatenate([s_re, s_im], axis=0)
    left_im = jnp.concatenate([s_im, -s_re], axis=0)
    cross_re = jnp.einsum('fks,fkc->ksc', left_re, right, precision=lax.Precision.HIGHEST)
    cross_im = jnp.einsum('fks,fkc->ksc', left_im, right, precision=lax.Precision.HIGHEST)
    cross = jnp.concatenate([cross_re, cross_im], axis=0)
    lagged = jnp.einsum('lk,ksc->slc', lag_table(), cross, precision=lax.Precision.HIGHEST)
    return lagged * (1.0 / math.sqrt(FRAMES * NBIN))

def reference(raw, taps, offsets, sources, edges):
    white = whiten(raw, taps, edges)
    mask = band_mask(edges)
    band_scale = 1.0 / jnp.sqrt(FRAMES * lax.optimization_barrier(jnp.sum(mask, axis=1)))

    def one_pair(offset):
        partner = jnp.roll(white, -offset, axis=2)
        return band_cross(white, partner, mask, band_scale)
    coherence = lax.map(one_pair, offsets)
    source_white = jnp.take(white, sources, axis=2)
    blocks = white.reshape(FRAMES, NFFT, N_CH, CH_DEV).transpose(2, 0, 1, 3)
    lagged = lax.map(lambda block: correlate(source_white, block), blocks)
    correlation = lagged.transpose(1, 2, 0, 3).reshape(SOURCES, LAGS, NCH)
    return (coherence, correlation)
```

```python
import math

import jax
import jax.numpy as jnp
import numpy as np
from jax import lax
from jax.experimental import pallas as pl
from jax.experimental.pallas import tpu as pltpu
from jax.sharding import PartitionSpec as P

SAMPLES = 4096
TAPS = 16
NFFT = 256
FRAMES = 8
NBIN = 128
BANDS = 16
SOURCES = 32
OFFS = 16
MAXLAG = 64
LAGS = 129
LAG_ROWS = 144
WIDTH = 128
HALO = 16
SPAN = 2 * NFFT + HALO
CHUNK = 16
CHUNKS = NBIN // CHUNK
VMEM_LIMIT = 48 * 1024 * 1024
F32 = jnp.float32
BF16 = jnp.bfloat16


def dft_table():
    phase = np.arange(NBIN)[:, None] * np.arange(NFFT)[None, :] % NFFT * (2.0 * math.pi / NFFT)
    return np.concatenate([np.cos(phase), -np.sin(phase)], axis=0).astype(np.float32)


def lag_tables():
    lags = np.arange(LAGS) - MAXLAG
    phase = lags[:, None] * np.arange(NBIN)[None, :] % NFFT * (2.0 * math.pi / NFFT)
    table = np.concatenate([np.cos(phase), -np.sin(phase)], axis=1) / math.sqrt(FRAMES * NBIN)
    table = np.pad(table, ((0, LAG_ROWS - LAGS), (0, 0))).astype(np.float32)
    high = table.astype(BF16)
    low = (table - high.astype(np.float32)).astype(BF16)
    return np.concatenate([high, low], axis=0)


def split(x, parts):
    out = []
    for _ in range(parts):
        piece = lax.reduce_precision(x, 8, 7)
        out.append(piece.astype(BF16))
        x = x - piece
    return out


def filtered_table(taps):
    n = lax.broadcasted_iota(jnp.int32, (NFFT, SPAN), 0)
    i = lax.broadcasted_iota(jnp.int32, (NFFT, SPAN), 1)
    which = 2 * n + HALO - i
    spread = jnp.zeros((NFFT, SPAN), F32)
    for j in range(TAPS):
        spread = jnp.where(which == j, taps[j], spread)
    table = jnp.dot(jnp.asarray(dft_table()), spread, precision=lax.Precision.HIGHEST)
    return jnp.stack(split(table, 3))


def chunk_rows(white, c):
    rows = []
    for f in range(FRAMES):
        for part in range(2):
            start = part * NBIN + c * CHUNK
            rows.append(white[f, start : start + CHUNK, :])
    return rows


def whiten_kernel(table, raw, mask, counts, onehot, white, picked, spectrum):
    squares = jnp.zeros((NFFT, WIDTH), F32)
    for f in range(FRAMES):
        total = jnp.zeros((NFFT, WIDTH), F32)
        for part in range(3):
            if f == 0:
                total += jnp.dot(
                    table[part, :, HALO:], raw[: 2 * NFFT, :], preferred_element_type=F32
                )
            else:
                start = f * 2 * NFFT - HALO
                total += jnp.dot(
                    table[part], raw[start : start + SPAN, :], preferred_element_type=F32
                )
        spectrum[f] = total
        squares += total * total
    squares = squares[:NBIN] + squares[NBIN:]
    power = jnp.dot(mask[...], squares, precision=lax.Precision.HIGHEST) / counts[...]
    level = jnp.sqrt(power + 1e-06)
    per_bin = lax.dot_general(
        mask[...], level, (((0,), (0,)), ((), ())), precision=lax.Precision.HIGHEST
    )
    inverse = 1.0 / per_bin
    for f in range(FRAMES):
        white[f, :NBIN, :] = (spectrum[f, :NBIN, :] * inverse).astype(BF16)
        white[f, NBIN:, :] = (spectrum[f, NBIN:, :] * inverse).astype(BF16)
    for c in range(CHUNKS):
        rows = jnp.concatenate(chunk_rows(white, c), axis=0)
        found = lax.dot_general(
            onehot[...], rows, (((1,), (1,)), ((), ())), preferred_element_type=F32
        ).astype(BF16)
        picked[2 * c] = found[:, :WIDTH]
        picked[2 * c + 1] = found[:, WIDTH:]


def whiten(raw, taps, mask, onehot):
    counts = 2.0 * FRAMES * jnp.sum(mask, axis=1, keepdims=True)
    return pl.pallas_call(
        whiten_kernel,
        out_shape=(
            jax.ShapeDtypeStruct((FRAMES, NFFT, WIDTH), BF16),
            jax.ShapeDtypeStruct((2 * CHUNKS, SOURCES, WIDTH), BF16),
        ),
        scratch_shapes=[pltpu.VMEM((FRAMES, NFFT, WIDTH), F32)],
        compiler_params=pltpu.CompilerParams(vmem_limit_bytes=VMEM_LIMIT),
        name="whiten",
    )(filtered_table(taps), raw, mask, counts, onehot)


def coherence_kernel(offsets, mask, scale, own, near, far, out, ext, base, high, low):
    for f in range(FRAMES):
        base[f] = own[f].astype(F32)
        ext[0, f] = base[f]
        ext[1, f] = near[f].astype(F32)
        ext[2, f] = far[f].astype(F32)
    lane = lax.broadcasted_iota(jnp.int32, (1, WIDTH), 1)
    step = 32

    def pair(p, _):
        offset = offsets[p]
        first = offset // WIDTH
        second = jnp.minimum(first + 1, 2)
        turn = offset % WIDTH
        wrapped = jnp.broadcast_to(lane < turn, (step, WIDTH))
        shift = (WIDTH - turn) % WIDTH

        def partner(f, start):
            a = ext[first, f, start : start + step, :]
            b = ext[second, f, start : start + step, :]
            return pltpu.roll(jnp.where(wrapped, b, a), shift, 1)

        for k in range(0, NBIN, step):
            real = jnp.zeros((step, WIDTH), F32)
            imag = jnp.zeros((step, WIDTH), F32)
            for f in range(FRAMES):
                p_re, p_im = partner(f, k), partner(f, NBIN + k)
                w_re = base[f, k : k + step, :]
                w_im = base[f, NBIN + k : NBIN + k + step, :]
                real += w_re * p_re + w_im * p_im
                imag += w_im * p_re - w_re * p_im
            for part, cross in enumerate((real, imag)):
                top = cross.astype(BF16)
                high[p, part, k : k + step, :] = top
                low[p, part, k : k + step, :] = (cross - top.astype(F32)).astype(BF16)
        return 0

    lax.fori_loop(0, OFFS, pair, 0)
    bands = mask[...].astype(BF16)
    for p in range(OFFS):
        for part in range(2):
            total = jnp.dot(bands, high[p, part], preferred_element_type=F32)
            total += jnp.dot(bands, low[p, part], preferred_element_type=F32)
            out[p, part * BANDS : (part + 1) * BANDS, :] = total * scale[...]


def coherences(offsets, mask, own, near, far):
    scale = 1.0 / jnp.sqrt(FRAMES * jnp.sum(mask, axis=1, keepdims=True))
    vmem = pl.BlockSpec(memory_space=pltpu.VMEM)
    return pl.pallas_call(
        coherence_kernel,
        out_shape=jax.ShapeDtypeStruct((OFFS, 2 * BANDS, WIDTH), F32),
        in_specs=[pl.BlockSpec(memory_space=pltpu.SMEM)] + [vmem] * 5,
        out_specs=vmem,
        scratch_shapes=[
            pltpu.VMEM((3, FRAMES, NFFT, WIDTH), F32),
            pltpu.VMEM((FRAMES, NFFT, WIDTH), F32),
            pltpu.VMEM((OFFS, 2, NBIN, WIDTH), BF16),
            pltpu.VMEM((OFFS, 2, NBIN, WIDTH), BF16),
        ],
        compiler_params=pltpu.CompilerParams(vmem_limit_bytes=VMEM_LIMIT),
        name="coherence",
    )(offsets, mask, scale, own, near, far)


S_STEP = 4


def correlate_kernel(table, sources, white, out, left, high, low):
    @pl.when(pl.program_id(0) == 0)
    def _():
        row = lax.broadcasted_iota(jnp.int32, (CHUNK, NFFT), 0)
        column = lax.broadcasted_iota(jnp.int32, (CHUNK, NFFT), 1)
        diagonal = (column % CHUNK) == row
        for c in range(CHUNKS):
            values = jnp.concatenate([sources[2 * c], sources[2 * c + 1]], axis=1).astype(F32)
            for s in range(SOURCES):
                spread = jnp.broadcast_to(values[s : s + 1, :], (CHUNK, NFFT))
                left[s * CHUNK : (s + 1) * CHUNK, :] = jnp.where(diagonal, spread, 0.0).astype(BF16)
            rows = chunk_rows(white, c)
            turned = []
            for f in range(FRAMES):
                turned += [-rows[2 * f + 1], rows[2 * f]]
            right = jnp.concatenate(
                [jnp.concatenate(rows, axis=0), jnp.concatenate(turned, axis=0)], axis=1
            )
            cross = jnp.dot(left[...], right, preferred_element_type=F32)
            top = cross.astype(BF16)
            rest = (cross - top.astype(F32)).astype(BF16)
            for kept, value in ((high, top), (low, rest)):
                value = value.reshape(SOURCES, CHUNK, 2 * WIDTH)
                for part in range(2):
                    start = part * NBIN + c * CHUNK
                    kept[:, start : start + CHUNK, :] = value[:, :, part * WIDTH : (part + 1) * WIDTH]

    base = pl.program_id(0) * S_STEP
    for i in range(0, S_STEP, 2):
        top = jnp.concatenate([high[base + i], high[base + i + 1]], axis=1)
        rest = jnp.concatenate([low[base + i], low[base + i + 1]], axis=1)
        both = jnp.dot(table[...], top, preferred_element_type=F32)
        lagged = both[:LAG_ROWS] + both[LAG_ROWS:]
        lagged += jnp.dot(table[:LAG_ROWS, :], rest, preferred_element_type=F32)
        out[i] = lagged[:LAGS, :WIDTH]
        out[i + 1] = lagged[:LAGS, WIDTH:]


def correlations(sources, white):
    return pl.pallas_call(
        correlate_kernel,
        grid=(SOURCES // S_STEP,),
        out_shape=jax.ShapeDtypeStruct((SOURCES, LAGS, WIDTH), F32),
        in_specs=[
            pl.BlockSpec((2 * LAG_ROWS, NFFT), lambda g: (0, 0)),
            pl.BlockSpec((2 * CHUNKS, SOURCES, WIDTH), lambda g: (0, 0, 0)),
            pl.BlockSpec((FRAMES, NFFT, WIDTH), lambda g: (0, 0, 0)),
        ],
        out_specs=pl.BlockSpec((S_STEP, LAGS, WIDTH), lambda g: (g, 0, 0)),
        scratch_shapes=[
            pltpu.VMEM((SOURCES * CHUNK, NFFT), BF16),
            pltpu.VMEM((SOURCES, NFFT, WIDTH), BF16),
            pltpu.VMEM((SOURCES, NFFT, WIDTH), BF16),
        ],
        compiler_params=pltpu.CompilerParams(vmem_limit_bytes=VMEM_LIMIT),
        name="correlate",
    )(jnp.asarray(lag_tables()), sources, white)


def from_behind(block, axis, distance):
    devices = range(lax.axis_size(axis))
    route = [((i - distance) % len(devices), i) for i in devices]
    return lax.ppermute(block, axis, route)


def groups_of(size, inner):
    if inner:
        return [list(range(g * inner, (g + 1) * inner)) for g in range(size // inner)]
    return [list(range(g, size, 16)) for g in range(16)]


def spread_sources(picked):
    size = lax.axis_size("ch")
    runs = groups_of(size, 16)
    places = groups_of(size, 0)
    mine = lax.all_to_all(picked, "ch", 0, 0, axis_index_groups=runs, tiled=True)
    mine = jnp.sum(mine.astype(F32), axis=0).astype(BF16)
    copies = jnp.broadcast_to(mine[None], (len(places[0]),) + mine.shape)
    mine = lax.all_to_all(copies, "ch", 0, 0, axis_index_groups=places, tiled=True)
    mine = jnp.sum(mine.astype(F32), axis=0).astype(BF16)
    copies = jnp.broadcast_to(mine[None], (len(runs[0]),) + mine.shape)
    return lax.all_to_all(copies, "ch", 0, 0, axis_index_groups=runs, tiled=True)


def per_device(raw, taps, offsets, sources, edges):
    bins = jnp.arange(NBIN, dtype=jnp.int32)
    mask = ((bins[None, :] >= edges[:-1, None]) & (bins[None, :] < edges[1:, None])).astype(F32)
    owned = lax.axis_index("ch") * WIDTH + jnp.arange(WIDTH, dtype=jnp.int32)
    onehot = (sources[:, None] == owned[None, :]).astype(BF16)
    white, picked = whiten(raw, taps, mask, onehot)
    near = from_behind(white, "ch", -1)
    far = from_behind(white, "ch", -2)
    coherence = coherences(offsets, mask, white, near, far)
    correlation = correlations(spread_sources(picked), white)
    return (coherence, correlation)


def solution(mesh):
    in_specs = (P(None, "ch"), P(), P(), P(), P())
    out_specs = (P(None, None, "ch"), P(None, None, "ch"))
    return jax.shard_map(
        per_device, mesh=mesh, in_specs=in_specs, out_specs=out_specs, check_vma=False
    )
```

```python
import math

import jax
import jax.numpy as jnp
import numpy as np
from jax import lax
from jax.experimental import pallas as pl
from jax.experimental.pallas import tpu as pltpu
from jax.sharding import PartitionSpec as P

SAMPLES = 4096
TAPS = 16
NFFT = 256
FRAMES = 8
NBIN = 128
BANDS = 16
SOURCES = 32
OFFS = 16
MAXLAG = 64
LAGS = 129
LAG_ROWS = 144
WIDTH = 128
HALO = 16
SPAN = 2 * NFFT + HALO
SPAN_LANES = 640
CHUNK = 16
CHUNKS = NBIN // CHUNK
VMEM_LIMIT = 48 * 1024 * 1024
F32 = jnp.float32
BF16 = jnp.bfloat16


def dft_table():
    phase = np.arange(NBIN)[:, None] * np.arange(NFFT)[None, :] % NFFT * (2.0 * math.pi / NFFT)
    return np.concatenate([np.cos(phase), -np.sin(phase)], axis=0).astype(np.float32)


def lag_tables():
    lags = np.arange(LAGS) - MAXLAG
    phase = lags[:, None] * np.arange(NBIN)[None, :] % NFFT * (2.0 * math.pi / NFFT)
    table = np.concatenate([np.cos(phase), -np.sin(phase)], axis=1) / math.sqrt(FRAMES * NBIN)
    table = np.pad(table, ((0, LAG_ROWS - LAGS), (0, 0))).astype(np.float32)
    high = table.astype(BF16)
    low = (table - high.astype(np.float32)).astype(BF16)
    return np.concatenate([high, low], axis=0)


def chunk_rows(white, c):
    rows = []
    for f in range(FRAMES):
        for part in range(2):
            start = part * NBIN + c * CHUNK
            rows.append(white[f, start : start + CHUNK, :])
    return rows


def band_masks(edges):
    band = lax.broadcasted_iota(jnp.int32, (BANDS, NBIN), 0)
    bins = lax.broadcasted_iota(jnp.int32, (BANDS, NBIN), 1)
    lowest = jnp.zeros((BANDS, NBIN), jnp.int32)
    limit = jnp.zeros((BANDS, NBIN), jnp.int32)
    for b in range(BANDS):
        lowest = jnp.where(band == b, edges[b], lowest)
        limit = jnp.where(band == b, edges[b + 1], limit)
    mask = jnp.where((bins >= lowest) & (bins < limit), 1.0, 0.0).astype(F32)
    return mask, (limit - lowest).astype(F32)


def filtered_table(taps, dft, spread, table):
    rows = 32
    spread[...] = jnp.zeros((NFFT, SPAN_LANES), F32)
    for start in range(0, NFFT, rows):
        left = (2 * start + 1) // WIDTH * WIDTH
        n = start + lax.broadcasted_iota(jnp.int32, (rows, 2 * WIDTH), 0)
        i = left + lax.broadcasted_iota(jnp.int32, (rows, 2 * WIDTH), 1)
        which = 2 * n + HALO - i
        block = jnp.zeros((rows, 2 * WIDTH), F32)
        for j in range(TAPS):
            block = jnp.where(which == j, taps[j], block)
        spread[start : start + rows, left : left + 2 * WIDTH] = block
    rest = jnp.dot(dft[...], spread[...], precision=lax.Precision.HIGHEST)
    for part in range(3):
        piece = rest.astype(BF16)
        table[part] = piece
        rest = rest - piece.astype(F32)


def whiten_kernel(first, taps, edges, sources, dft, raw, white, picked, spread, table, spectrum):
    filtered_table(taps, dft, spread, table)
    squares = jnp.zeros((NFFT, WIDTH), F32)
    for f in range(FRAMES):
        total = jnp.zeros((NFFT, WIDTH), F32)
        for part in range(3):
            if f == 0:
                total += jnp.dot(
                    table[part, :, HALO:SPAN], raw[: 2 * NFFT, :], preferred_element_type=F32
                )
            else:
                start = f * 2 * NFFT - HALO
                total += jnp.dot(
                    table[part, :, :SPAN], raw[start : start + SPAN, :], preferred_element_type=F32
                )
        spectrum[f] = total
        squares += total * total
    squares = squares[:NBIN] + squares[NBIN:]
    mask, bins = band_masks(edges)
    power = jnp.dot(mask, squares, precision=lax.Precision.HIGHEST) / (2.0 * FRAMES * bins)
    level = jnp.sqrt(power + 1e-06)
    per_bin = lax.dot_general(
        mask, level, (((0,), (0,)), ((), ())), precision=lax.Precision.HIGHEST
    )
    inverse = 1.0 / per_bin
    for f in range(FRAMES):
        white[f, :NBIN, :] = (spectrum[f, :NBIN, :] * inverse).astype(BF16)
        white[f, NBIN:, :] = (spectrum[f, NBIN:, :] * inverse).astype(BF16)
    which = lax.broadcasted_iota(jnp.int32, (SOURCES, WIDTH), 0)
    channel = first[0] + lax.broadcasted_iota(jnp.int32, (SOURCES, WIDTH), 1)
    wanted = jnp.zeros((SOURCES, WIDTH), jnp.int32)
    for s in range(SOURCES):
        wanted = jnp.where(which == s, sources[s], wanted)
    onehot = jnp.where(wanted == channel, 1.0, 0.0).astype(BF16)
    for c in range(CHUNKS):
        rows = jnp.concatenate(chunk_rows(white, c), axis=0)
        found = lax.dot_general(
            onehot, rows, (((1,), (1,)), ((), ())), preferred_element_type=F32
        ).astype(BF16)
        picked[2 * c] = found[:, :WIDTH]
        picked[2 * c + 1] = found[:, WIDTH:]


SMEM = pl.BlockSpec(memory_space=pltpu.SMEM)
VMEM = pl.BlockSpec(memory_space=pltpu.VMEM)


def whiten(raw, taps, edges, sources, first):
    return pl.pallas_call(
        whiten_kernel,
        out_shape=(
            jax.ShapeDtypeStruct((FRAMES, NFFT, WIDTH), BF16),
            jax.ShapeDtypeStruct((2 * CHUNKS, SOURCES, WIDTH), BF16),
        ),
        in_specs=[SMEM] * 4 + [VMEM] * 2,
        out_specs=(VMEM, VMEM),
        scratch_shapes=[
            pltpu.VMEM((NFFT, SPAN_LANES), F32),
            pltpu.VMEM((3, NFFT, SPAN_LANES), BF16),
            pltpu.VMEM((FRAMES, NFFT, WIDTH), F32),
        ],
        compiler_params=pltpu.CompilerParams(vmem_limit_bytes=VMEM_LIMIT),
        name="whiten",
    )(first, taps, edges, sources, jnp.asarray(dft_table()), raw)


def coherence_kernel(offsets, edges, own, near, far, out, ext, base, high, low):
    for f in range(FRAMES):
        base[f] = own[f].astype(F32)
        ext[0, f] = own[f]
        ext[1, f] = near[f]
        ext[2, f] = far[f]
    lane = lax.broadcasted_iota(jnp.int32, (1, WIDTH), 1)
    step = 32

    def pair(p, _):
        offset = offsets[p]
        first = offset // WIDTH
        second = jnp.minimum(first + 1, 2)
        turn = offset % WIDTH
        wrapped = jnp.broadcast_to(lane < turn, (step, WIDTH))
        shift = (WIDTH - turn) % WIDTH

        def partner(f, start):
            a = ext[first, f, start : start + step, :]
            b = ext[second, f, start : start + step, :]
            return pltpu.roll(jnp.where(wrapped, b, a), shift, 1).astype(F32)

        for k in range(0, NBIN, step):
            real = jnp.zeros((step, WIDTH), F32)
            imag = jnp.zeros((step, WIDTH), F32)
            for f in range(FRAMES):
                p_re, p_im = partner(f, k), partner(f, NBIN + k)
                w_re = base[f, k : k + step, :]
                w_im = base[f, NBIN + k : NBIN + k + step, :]
                real += w_re * p_re + w_im * p_im
                imag += w_im * p_re - w_re * p_im
            for part, cross in enumerate((real, imag)):
                top = cross.astype(BF16)
                high[p, part, k : k + step, :] = top
                low[p, part, k : k + step, :] = (cross - top.astype(F32)).astype(BF16)
        return 0

    lax.fori_loop(0, OFFS, pair, 0)
    mask, bins = band_masks(edges)
    scale = 1.0 / jnp.sqrt(FRAMES * bins)
    bands = mask.astype(BF16)
    for p in range(OFFS):
        for part in range(2):
            total = jnp.dot(bands, high[p, part], preferred_element_type=F32)
            total += jnp.dot(bands, low[p, part], preferred_element_type=F32)
            out[p, part * BANDS : (part + 1) * BANDS, :] = total * scale


def coherences(offsets, edges, own, near, far):
    return pl.pallas_call(
        coherence_kernel,
        out_shape=jax.ShapeDtypeStruct((OFFS, 2 * BANDS, WIDTH), F32),
        in_specs=[SMEM] * 2 + [VMEM] * 3,
        out_specs=VMEM,
        scratch_shapes=[
            pltpu.VMEM((3, FRAMES, NFFT, WIDTH), BF16),
            pltpu.VMEM((FRAMES, NFFT, WIDTH), F32),
            pltpu.VMEM((OFFS, 2, NBIN, WIDTH), BF16),
            pltpu.VMEM((OFFS, 2, NBIN, WIDTH), BF16),
        ],
        compiler_params=pltpu.CompilerParams(vmem_limit_bytes=VMEM_LIMIT),
        name="coherence",
    )(offsets, edges, own, near, far)


S_STEP = 8


def correlate_kernel(table, sources, white, out, left, high, low):
    @pl.when(pl.program_id(0) == 0)
    def _():
        row = lax.broadcasted_iota(jnp.int32, (CHUNK, NFFT), 0)
        column = lax.broadcasted_iota(jnp.int32, (CHUNK, NFFT), 1)
        diagonal = (column % CHUNK) == row
        for c in range(CHUNKS):
            values = jnp.concatenate([sources[2 * c], sources[2 * c + 1]], axis=1).astype(F32)
            for s in range(SOURCES):
                spread = jnp.broadcast_to(values[s : s + 1, :], (CHUNK, NFFT))
                left[s * CHUNK : (s + 1) * CHUNK, :] = jnp.where(diagonal, spread, 0.0).astype(BF16)
            rows = chunk_rows(white, c)
            turned = []
            for f in range(FRAMES):
                turned += [-rows[2 * f + 1], rows[2 * f]]
            right = jnp.concatenate(
                [jnp.concatenate(rows, axis=0), jnp.concatenate(turned, axis=0)], axis=1
            )
            cross = jnp.dot(left[...], right, preferred_element_type=F32)
            top = cross.astype(BF16)
            rest = (cross - top.astype(F32)).astype(BF16)
            for kept, value in ((high, top), (low, rest)):
                value = value.reshape(SOURCES, CHUNK, 2 * WIDTH)
                for part in range(2):
                    start = part * NBIN + c * CHUNK
                    kept[:, start : start + CHUNK, :] = value[:, :, part * WIDTH : (part + 1) * WIDTH]

    base = pl.program_id(0) * S_STEP
    for i in range(0, S_STEP, 2):
        top = jnp.concatenate([high[base + i], high[base + i + 1]], axis=1)
        rest = jnp.concatenate([low[base + i], low[base + i + 1]], axis=1)
        both = jnp.dot(table[...], top, preferred_element_type=F32)
        lagged = both[:LAG_ROWS] + both[LAG_ROWS:]
        lagged += jnp.dot(table[:LAG_ROWS, :], rest, preferred_element_type=F32)
        out[:, i, :] = lagged[:LAGS, :WIDTH]
        out[:, i + 1, :] = lagged[:LAGS, WIDTH:]


def correlations(sources, white):
    return pl.pallas_call(
        correlate_kernel,
        grid=(SOURCES // S_STEP,),
        out_shape=jax.ShapeDtypeStruct((LAGS, SOURCES, WIDTH), F32),
        in_specs=[
            pl.BlockSpec((2 * LAG_ROWS, NFFT), lambda g: (0, 0)),
            pl.BlockSpec((2 * CHUNKS, SOURCES, WIDTH), lambda g: (0, 0, 0)),
            pl.BlockSpec((FRAMES, NFFT, WIDTH), lambda g: (0, 0, 0)),
        ],
        out_specs=pl.BlockSpec((LAGS, S_STEP, WIDTH), lambda g: (0, g, 0)),
        scratch_shapes=[
            pltpu.VMEM((SOURCES * CHUNK, NFFT), BF16),
            pltpu.VMEM((SOURCES, NFFT, WIDTH), BF16),
            pltpu.VMEM((SOURCES, NFFT, WIDTH), BF16),
        ],
        compiler_params=pltpu.CompilerParams(vmem_limit_bytes=VMEM_LIMIT),
        name="correlate",
    )(jnp.asarray(lag_tables()), sources, white).transpose(1, 0, 2)


def from_behind(block, axis, distance):
    devices = range(lax.axis_size(axis))
    route = [((i - distance) % len(devices), i) for i in devices]
    return lax.ppermute(block, axis, route)


def groups_of(size, inner):
    if inner:
        return [list(range(g * inner, (g + 1) * inner)) for g in range(size // inner)]
    return [list(range(g, size, 16)) for g in range(16)]


def spread_sources(picked):
    size = lax.axis_size("ch")
    runs = groups_of(size, 16)
    places = groups_of(size, 0)
    mine = lax.all_to_all(picked, "ch", 0, 0, axis_index_groups=runs, tiled=True)
    mine = jnp.sum(mine.astype(F32), axis=0).astype(BF16)
    copies = jnp.broadcast_to(mine[None], (len(places[0]),) + mine.shape)
    mine = lax.all_to_all(copies, "ch", 0, 0, axis_index_groups=places, tiled=True)
    mine = jnp.sum(mine.astype(F32), axis=0).astype(BF16)
    copies = jnp.broadcast_to(mine[None], (len(runs[0]),) + mine.shape)
    return lax.all_to_all(copies, "ch", 0, 0, axis_index_groups=runs, tiled=True)


def per_device(raw, taps, offsets, sources, edges):
    first = jnp.full((1,), lax.axis_index("ch") * WIDTH, jnp.int32)
    white, picked = whiten(raw, taps, edges, sources, first)
    near = from_behind(white, "ch", -1)
    far = from_behind(white, "ch", -2)
    coherence = coherences(offsets, edges, white, near, far)
    correlation = correlations(spread_sources(picked), white)
    return (coherence, correlation)


def solution(mesh):
    in_specs = (P(None, "ch"), P(), P(), P(), P())
    out_specs = (P(None, None, "ch"), P(None, None, "ch"))
    return jax.shard_map(
        per_device, mesh=mesh, in_specs=in_specs, out_specs=out_specs, check_vma=False
    )
```

```python
import math

import jax
import jax.numpy as jnp
import numpy as np
from jax import lax
from jax.experimental import pallas as pl
from jax.experimental.pallas import tpu as pltpu
from jax.sharding import PartitionSpec as P

SAMPLES = 4096
TAPS = 16
NFFT = 256
FRAMES = 8
NBIN = 128
BANDS = 16
SOURCES = 32
OFFS = 16
MAXLAG = 64
LAGS = 129
LAG_ROWS = 144
WIDTH = 128
HALO = 16
SPAN = 2 * NFFT + HALO
SPAN_LANES = 640
CHUNK = 16
CHUNKS = NBIN // CHUNK
RUN = 16
VMEM_LIMIT = 48 * 1024 * 1024
F32 = jnp.float32
BF16 = jnp.bfloat16


def turn_tables():
    sample = np.arange(SPAN)[None, :] - HALO
    bins = np.arange(NBIN)[:, None]
    phase = bins * sample % (2 * NFFT) * (math.pi / NFFT)
    turns = np.stack([np.cos(phase), np.sin(phase)]).astype(np.float32)
    turns = np.pad(turns, ((0, 0), (0, 0), (0, SPAN_LANES - SPAN)))
    phase = bins * np.arange(TAPS)[None, :] % (2 * NFFT) * (math.pi / NFFT)
    return turns, np.concatenate([np.cos(phase), -np.sin(phase)], axis=0).astype(np.float32)


def lag_tables():
    lags = np.arange(LAGS) - MAXLAG
    phase = lags[:, None] * np.arange(NBIN)[None, :] % NFFT * (2.0 * math.pi / NFFT)
    table = np.concatenate([np.cos(phase), -np.sin(phase)], axis=1) / math.sqrt(FRAMES * NBIN)
    table = np.pad(table, ((0, LAG_ROWS - LAGS), (0, 0))).astype(np.float32)
    high = table.astype(BF16)
    low = (table - high.astype(np.float32)).astype(BF16)
    return np.concatenate([high, low], axis=0)


def chunk_rows(white, c):
    rows = []
    for f in range(FRAMES):
        for part in range(2):
            start = part * NBIN + c * CHUNK
            rows.append(white[f, start : start + CHUNK, :])
    return rows


def band_masks(edges):
    band = lax.broadcasted_iota(jnp.int32, (BANDS, NBIN), 0)
    bins = lax.broadcasted_iota(jnp.int32, (BANDS, NBIN), 1)
    lowest = jnp.zeros((BANDS, NBIN), jnp.int32)
    limit = jnp.zeros((BANDS, NBIN), jnp.int32)
    for b in range(BANDS):
        lowest = jnp.where(band == b, edges[b], lowest)
        limit = jnp.where(band == b, edges[b + 1], limit)
    mask = jnp.where((bins >= lowest) & (bins < limit), 1.0, 0.0).astype(F32)
    return mask, (limit - lowest).astype(F32)


def filtered_table(taps, turns, tap_turns, table):
    tap = lax.broadcasted_iota(jnp.int32, (TAPS, WIDTH), 0)
    lane = lax.broadcasted_iota(jnp.int32, (TAPS, WIDTH), 1)
    value = jnp.zeros((TAPS, WIDTH), F32)
    for j in range(TAPS):
        value = jnp.where(tap == j, taps[j], value)
    value = jnp.where((lane + tap) % 2 == 0, value, 0.0)
    early = jnp.where(lane + tap >= HALO, value, 0.0)
    late = jnp.where(lane + tap < HALO, value, 0.0)
    meets = jnp.concatenate([early, value, late], axis=1)
    response = jnp.dot(tap_turns[...], meets, precision=lax.Precision.HIGHEST)
    for block in range(SPAN_LANES // WIDTH):
        lanes = slice(block * WIDTH, (block + 1) * WIDTH)
        kind = 0 if block == 0 else 2 if block == SPAN_LANES // WIDTH - 1 else 1
        re = response[:NBIN, kind * WIDTH : (kind + 1) * WIDTH]
        im = response[NBIN:, kind * WIDTH : (kind + 1) * WIDTH]
        cos, sin = turns[0, :, lanes], turns[1, :, lanes]
        for half, rest in enumerate((cos * re + sin * im, cos * im - sin * re)):
            for part in range(3):
                piece = rest.astype(BF16)
                row = part * NFFT + half * NBIN
                table[row : row + NBIN, lanes] = piece
                rest = rest - piece.astype(F32)


def whiten_kernel(
    first, taps_hbm, edges_hbm, sources_hbm, turns_hbm, tap_turns_hbm, raw_hbm,
    white, picked,
    taps, edges, sources, turns, tap_turns, raw, table, spectrum, sems,
):
    loads = [
        pltpu.make_async_copy(src, dst, sems.at[i])
        for i, (src, dst) in enumerate(
            (
                (taps_hbm, taps),
                (tap_turns_hbm, tap_turns),
                (turns_hbm, turns),
                (raw_hbm, raw),
                (edges_hbm, edges),
                (sources_hbm, sources),
            )
        )
    ]
    for load in loads:
        load.start()
    for load in loads[:3]:
        load.wait()
    filtered_table(taps, turns, tap_turns, table)
    for load in loads[3:]:
        load.wait()
    squares = jnp.zeros((NFFT, WIDTH), F32)
    halo = [jnp.zeros((HALO, WIDTH), BF16)]
    halo += [raw[f * 2 * NFFT - HALO : f * 2 * NFFT, :] for f in range(1, FRAMES)]
    for f in range(0, FRAMES, 2):
        pair = [
            jnp.concatenate([halo[g], raw[g * 2 * NFFT : (g + 1) * 2 * NFFT, :]], axis=0)
            for g in (f, f + 1)
        ]
        parts = jnp.dot(
            table[:, :SPAN], jnp.concatenate(pair, axis=1), preferred_element_type=F32
        )
        both = parts[:NFFT] + parts[NFFT : 2 * NFFT] + parts[2 * NFFT :]
        for g in range(2):
            total = both[:, g * WIDTH : (g + 1) * WIDTH]
            spectrum[f + g] = total
            squares += total * total
    squares = squares[:NBIN] + squares[NBIN:]
    mask, bins = band_masks(edges)
    power = jnp.dot(mask, squares, precision=lax.Precision.HIGHEST) / (2.0 * FRAMES * bins)
    level = jnp.sqrt(power + 1e-06)
    per_bin = lax.dot_general(
        mask, level, (((0,), (0,)), ((), ())), precision=lax.Precision.HIGHEST
    )
    inverse = 1.0 / per_bin
    for f in range(FRAMES):
        white[f, :NBIN, :] = (spectrum[f, :NBIN, :] * inverse).astype(BF16)
        white[f, NBIN:, :] = (spectrum[f, NBIN:, :] * inverse).astype(BF16)
    which = lax.broadcasted_iota(jnp.int32, (SOURCES, WIDTH), 0)
    channel = first[0] + lax.broadcasted_iota(jnp.int32, (SOURCES, WIDTH), 1)
    wanted = jnp.zeros((SOURCES, WIDTH), jnp.int32)
    for s in range(SOURCES):
        wanted = jnp.where(which == s, sources[s], wanted)
    onehot = jnp.where(wanted == channel, 1.0, 0.0).astype(BF16)
    for c in range(CHUNKS):
        rows = jnp.concatenate(chunk_rows(white, c), axis=0)
        found = lax.dot_general(
            onehot, rows, (((1,), (1,)), ((), ())), preferred_element_type=F32
        ).astype(BF16)
        picked[2 * c] = found[:, :WIDTH]
        picked[2 * c + 1] = found[:, WIDTH:]


SMEM = pl.BlockSpec(memory_space=pltpu.SMEM)
VMEM = pl.BlockSpec(memory_space=pltpu.VMEM)


def whiten(raw, taps, edges, sources, first):
    turns, tap_turns = turn_tables()
    return pl.pallas_call(
        whiten_kernel,
        out_shape=(
            jax.ShapeDtypeStruct((FRAMES, NFFT, WIDTH), BF16),
            jax.ShapeDtypeStruct((2 * CHUNKS, SOURCES, WIDTH), BF16),
        ),
        in_specs=[SMEM] + [pl.BlockSpec(memory_space=pl.ANY)] * 6,
        out_specs=(VMEM, VMEM),
        scratch_shapes=[
            pltpu.SMEM((TAPS,), F32),
            pltpu.SMEM((BANDS + 1,), jnp.int32),
            pltpu.SMEM((SOURCES,), jnp.int32),
            pltpu.VMEM((2, NBIN, SPAN_LANES), F32),
            pltpu.VMEM((NFFT, TAPS), F32),
            pltpu.VMEM((SAMPLES, WIDTH), BF16),
            pltpu.VMEM((3 * NFFT, SPAN_LANES), BF16),
            pltpu.VMEM((FRAMES, NFFT, WIDTH), F32),
            pltpu.SemaphoreType.DMA((6,)),
        ],
        name="whiten",
    )(first, taps, edges, sources, jnp.asarray(turns), jnp.asarray(tap_turns), raw)


def coherence_kernel(offsets, edges, own, near, far, out, ext, high, low):
    for f in range(FRAMES):
        ext[0, f] = own[f]
        ext[1, f] = near[f]
        ext[2, f] = far[f]
    lane = lax.broadcasted_iota(jnp.int32, (1, WIDTH), 1)
    step = 16

    def place(offset):
        first = offset // WIDTH
        turn = offset % WIDTH
        wrapped = jnp.broadcast_to(lane < turn, (step, WIDTH))
        return first, jnp.minimum(first + 1, 2), wrapped, (WIDTH - turn) % WIDTH

    def partner(where, f, start):
        first, second, wrapped, shift = where
        a = ext[first, f, start : start + step, :]
        b = ext[second, f, start : start + step, :]
        return pltpu.roll(jnp.where(wrapped, b, a), shift, 1).astype(F32)

    def pairs(i, _):
        places = [place(offsets[4 * i + n]) for n in range(4)]
        for k in range(0, NBIN, step):
            real = [jnp.zeros((step, WIDTH), F32) for _ in places]
            imag = [jnp.zeros((step, WIDTH), F32) for _ in places]
            for f in range(FRAMES):
                w_re = own[f, k : k + step, :].astype(F32)
                w_im = own[f, NBIN + k : NBIN + k + step, :].astype(F32)
                for n, where in enumerate(places):
                    p_re, p_im = partner(where, f, k), partner(where, f, NBIN + k)
                    real[n] += w_re * p_re + w_im * p_im
                    imag[n] += w_im * p_re - w_re * p_im
            for n in range(4):
                for part, cross in enumerate((real[n], imag[n])):
                    top = cross.astype(BF16)
                    high[4 * i + n, part, k : k + step, :] = top
                    low[4 * i + n, part, k : k + step, :] = (cross - top.astype(F32)).astype(BF16)
        return 0

    lax.fori_loop(0, OFFS // 4, pairs, 0)
    mask, bins = band_masks(edges)
    scale = 1.0 / jnp.sqrt(FRAMES * bins)
    bands = mask.astype(BF16)
    weights = jnp.concatenate([bands, bands], axis=1)
    for p in range(OFFS):
        real = jnp.concatenate([high[p, 0], low[p, 0]], axis=0)
        imag = jnp.concatenate([high[p, 1], low[p, 1]], axis=0)
        total = jnp.dot(
            weights, jnp.concatenate([real, imag], axis=1), preferred_element_type=F32
        )
        out[p, :BANDS, :] = total[:, :WIDTH] * scale
        out[p, BANDS:, :] = total[:, WIDTH:] * scale


def coherences(offsets, edges, own, near, far):
    return pl.pallas_call(
        coherence_kernel,
        out_shape=jax.ShapeDtypeStruct((OFFS, 2 * BANDS, WIDTH), F32),
        in_specs=[SMEM] * 2 + [VMEM] * 3,
        out_specs=VMEM,
        scratch_shapes=[
            pltpu.VMEM((3, FRAMES, NFFT, WIDTH), BF16),
            pltpu.VMEM((OFFS, 2, NBIN, WIDTH), BF16),
            pltpu.VMEM((OFFS, 2, NBIN, WIDTH), BF16),
        ],
        compiler_params=pltpu.CompilerParams(vmem_limit_bytes=VMEM_LIMIT),
        name="coherence",
    )(offsets, edges, own, near, far)


S_STEP = 8


def correlate_kernel(table, sources, white, out, left, high, low):
    @pl.when(pl.program_id(0) == 0)
    def _():
        row = lax.broadcasted_iota(jnp.int32, (CHUNK, NFFT), 0)
        column = lax.broadcasted_iota(jnp.int32, (CHUNK, NFFT), 1)
        diagonal = (column % CHUNK) == row
        for c in range(CHUNKS):
            values = jnp.concatenate([sources[2 * c], sources[2 * c + 1]], axis=1).astype(F32)
            for s in range(SOURCES):
                spread = jnp.broadcast_to(values[s : s + 1, :], (CHUNK, NFFT))
                left[s * CHUNK : (s + 1) * CHUNK, :] = jnp.where(diagonal, spread, 0.0).astype(BF16)
            rows = chunk_rows(white, c)
            turned = []
            for f in range(FRAMES):
                turned += [-rows[2 * f + 1], rows[2 * f]]
            right = jnp.concatenate(
                [jnp.concatenate(rows, axis=0), jnp.concatenate(turned, axis=0)], axis=1
            )
            cross = jnp.dot(left[...], right, preferred_element_type=F32)
            top = cross.astype(BF16)
            rest = (cross - top.astype(F32)).astype(BF16)
            for kept, value in ((high, top), (low, rest)):
                value = value.reshape(SOURCES, CHUNK, 2 * WIDTH)
                for part in range(2):
                    start = part * NBIN + c * CHUNK
                    kept[:, start : start + CHUNK, :] = value[:, :, part * WIDTH : (part + 1) * WIDTH]

    base = pl.program_id(0) * S_STEP
    for i in range(0, S_STEP, 2):
        top = jnp.concatenate([high[base + i], high[base + i + 1]], axis=1)
        rest = jnp.concatenate([low[base + i], low[base + i + 1]], axis=1)
        both = jnp.dot(table[...], top, preferred_element_type=F32)
        lagged = both[:LAG_ROWS] + both[LAG_ROWS:]
        lagged += jnp.dot(table[:LAG_ROWS, :], rest, preferred_element_type=F32)
        out[:, i, :] = lagged[:LAGS, :WIDTH]
        out[:, i + 1, :] = lagged[:LAGS, WIDTH:]


def correlations(sources, white):
    return pl.pallas_call(
        correlate_kernel,
        grid=(SOURCES // S_STEP,),
        out_shape=jax.ShapeDtypeStruct((LAGS, SOURCES, WIDTH), F32),
        in_specs=[
            pl.BlockSpec((2 * LAG_ROWS, NFFT), lambda g: (0, 0)),
            pl.BlockSpec((2 * CHUNKS, SOURCES, WIDTH), lambda g: (0, 0, 0)),
            pl.BlockSpec((FRAMES, NFFT, WIDTH), lambda g: (0, 0, 0)),
        ],
        out_specs=pl.BlockSpec((LAGS, S_STEP, WIDTH), lambda g: (0, g, 0)),
        scratch_shapes=[
            pltpu.VMEM((SOURCES * CHUNK, NFFT), BF16),
            pltpu.VMEM((SOURCES, NFFT, WIDTH), BF16),
            pltpu.VMEM((SOURCES, NFFT, WIDTH), BF16),
        ],
        compiler_params=pltpu.CompilerParams(vmem_limit_bytes=VMEM_LIMIT),
        name="correlate",
    )(jnp.asarray(lag_tables()), sources, white).transpose(1, 0, 2)


def from_behind(block, axis, distance):
    devices = range(lax.axis_size(axis))
    route = [((i - distance) % len(devices), i) for i in devices]
    return lax.ppermute(block, axis, route)


def spread_sources(picked, work):
    size = lax.axis_size("ch")
    runs = [list(range(g, g + RUN)) for g in range(0, size, RUN)]
    places = [list(range(g, size, RUN)) for g in range(RUN)]
    shape = picked.shape
    mine = picked.reshape(RUN, -1, WIDTH)
    mine = lax.all_to_all(mine, "ch", 0, 0, axis_index_groups=runs, tiled=True)
    mine = jnp.sum(mine.astype(F32), axis=0).astype(BF16)
    copies = jnp.broadcast_to(mine[None], (size // RUN,) + mine.shape)
    mine = lax.all_to_all(copies, "ch", 0, 0, axis_index_groups=places, tiled=True)
    mine = jnp.sum(mine.astype(F32), axis=0).astype(BF16)
    mine, done = lax.optimization_barrier((mine, work()))
    copies = jnp.broadcast_to(mine[None], (RUN,) + mine.shape)
    found = lax.all_to_all(copies, "ch", 0, 0, axis_index_groups=runs, tiled=True)
    return done, found.reshape(shape)


def per_device(raw, taps, offsets, sources, edges):
    first = jnp.full((1,), lax.axis_index("ch") * WIDTH, jnp.int32)
    white, picked = whiten(raw, taps, edges, sources, first)
    near = from_behind(white, "ch", -1)
    far = from_behind(white, "ch", -2)
    (near, far), found = spread_sources(picked, lambda: (near, far))
    coherence = coherences(offsets, edges, white, near, far)
    correlation = correlations(found, white)
    return (coherence, correlation)


def solution(mesh):
    in_specs = (P(None, "ch"), P(), P(), P(), P())
    out_specs = (P(None, None, "ch"), P(None, None, "ch"))
    return jax.shard_map(
        per_device, mesh=mesh, in_specs=in_specs, out_specs=out_specs, check_vma=False
    )
```

```python
import math

import jax
import jax.numpy as jnp
import numpy as np
from jax import lax
from jax.experimental import pallas as pl
from jax.experimental.pallas import tpu as pltpu
from jax.sharding import PartitionSpec as P

SAMPLES = 4096
TAPS = 16
NFFT = 256
FRAMES = 8
NBIN = 128
BANDS = 16
SOURCES = 32
OFFS = 16
MAXLAG = 64
LAGS = 129
LAG_ROWS = 144
WIDTH = 128
HALO = 16
SPAN = 2 * NFFT + HALO
SPAN_LANES = 640
CHUNK = 16
CHUNKS = NBIN // CHUNK
RUN = 16
VMEM_LIMIT = 48 * 1024 * 1024
F32 = jnp.float32
BF16 = jnp.bfloat16


def turn_tables():
    sample = np.arange(SPAN)[None, :] - HALO
    bins = np.arange(NBIN)[:, None]
    phase = bins * sample % (2 * NFFT) * (math.pi / NFFT)
    turns = np.stack([np.cos(phase), np.sin(phase)]).astype(np.float32)
    turns = np.pad(turns, ((0, 0), (0, 0), (0, SPAN_LANES - SPAN)))
    phase = bins * np.arange(TAPS)[None, :] % (2 * NFFT) * (math.pi / NFFT)
    return turns, np.concatenate([np.cos(phase), -np.sin(phase)], axis=0).astype(np.float32)


def lag_tables():
    lags = np.arange(LAGS) - MAXLAG
    phase = lags[:, None] * np.arange(NBIN)[None, :] % NFFT * (2.0 * math.pi / NFFT)
    table = np.concatenate([np.cos(phase), -np.sin(phase)], axis=1) / math.sqrt(FRAMES * NBIN)
    table = np.pad(table, ((0, LAG_ROWS - LAGS), (0, 0))).astype(np.float32)
    high = table.astype(BF16)
    low = (table - high.astype(np.float32)).astype(BF16)
    return np.concatenate([high, low], axis=0)


def chunk_rows(white, c):
    rows = []
    for f in range(FRAMES):
        for part in range(2):
            start = part * NBIN + c * CHUNK
            rows.append(white[f, start : start + CHUNK, :])
    return rows


def band_masks(edges):
    band = lax.broadcasted_iota(jnp.int32, (BANDS, NBIN), 0)
    bins = lax.broadcasted_iota(jnp.int32, (BANDS, NBIN), 1)
    lowest = jnp.zeros((BANDS, NBIN), jnp.int32)
    limit = jnp.zeros((BANDS, NBIN), jnp.int32)
    for b in range(BANDS):
        lowest = jnp.where(band == b, edges[b], lowest)
        limit = jnp.where(band == b, edges[b + 1], limit)
    mask = jnp.where((bins >= lowest) & (bins < limit), 1.0, 0.0).astype(F32)
    return mask, (limit - lowest).astype(F32)


def filtered_table(taps, turns, tap_turns, table):
    tap = lax.broadcasted_iota(jnp.int32, (TAPS, WIDTH), 0)
    lane = lax.broadcasted_iota(jnp.int32, (TAPS, WIDTH), 1)
    value = jnp.zeros((TAPS, WIDTH), F32)
    for j in range(TAPS):
        value = jnp.where(tap == j, taps[j], value)
    value = jnp.where((lane + tap) % 2 == 0, value, 0.0)
    early = jnp.where(lane + tap >= HALO, value, 0.0)
    late = jnp.where(lane + tap < HALO, value, 0.0)
    meets = jnp.concatenate([early, value, late], axis=1)
    response = jnp.dot(tap_turns[...], meets, precision=lax.Precision.HIGHEST)
    for block in range(SPAN_LANES // WIDTH):
        lanes = slice(block * WIDTH, (block + 1) * WIDTH)
        kind = 0 if block == 0 else 2 if block == SPAN_LANES // WIDTH - 1 else 1
        re = response[:NBIN, kind * WIDTH : (kind + 1) * WIDTH]
        im = response[NBIN:, kind * WIDTH : (kind + 1) * WIDTH]
        cos, sin = turns[0, :, lanes], turns[1, :, lanes]
        for half, rest in enumerate((cos * re + sin * im, cos * im - sin * re)):
            for part in range(3):
                piece = rest.astype(BF16)
                row = part * NFFT + half * NBIN
                table[row : row + NBIN, lanes] = piece
                rest = rest - piece.astype(F32)


def whiten_kernel(
    first, taps_hbm, edges_hbm, sources_hbm, turns_hbm, tap_turns_hbm, raw_hbm,
    white, picked,
    taps, edges, sources, turns, tap_turns, raw, table, spectrum, sems,
):
    loads = [
        pltpu.make_async_copy(src, dst, sems.at[i])
        for i, (src, dst) in enumerate(
            (
                (taps_hbm, taps),
                (tap_turns_hbm, tap_turns),
                (turns_hbm, turns),
                (raw_hbm, raw),
                (edges_hbm, edges),
                (sources_hbm, sources),
            )
        )
    ]
    for load in loads:
        load.start()
    for load in loads[:3]:
        load.wait()
    filtered_table(taps, turns, tap_turns, table)
    for load in loads[3:]:
        load.wait()
    squares = jnp.zeros((NFFT, WIDTH), F32)
    halo = [jnp.zeros((HALO, WIDTH), BF16)]
    halo += [raw[f * 2 * NFFT - HALO : f * 2 * NFFT, :] for f in range(1, FRAMES)]
    for f in range(0, FRAMES, 2):
        pair = [
            jnp.concatenate([halo[g], raw[g * 2 * NFFT : (g + 1) * 2 * NFFT, :]], axis=0)
            for g in (f, f + 1)
        ]
        parts = jnp.dot(
            table[:, :SPAN], jnp.concatenate(pair, axis=1), preferred_element_type=F32
        )
        both = parts[:NFFT] + parts[NFFT : 2 * NFFT] + parts[2 * NFFT :]
        for g in range(2):
            total = both[:, g * WIDTH : (g + 1) * WIDTH]
            spectrum[f + g] = total
            squares += total * total
    squares = squares[:NBIN] + squares[NBIN:]
    mask, bins = band_masks(edges)
    power = jnp.dot(mask, squares, precision=lax.Precision.HIGHEST) / (2.0 * FRAMES * bins)
    level = jnp.sqrt(power + 1e-06)
    per_bin = lax.dot_general(
        mask, level, (((0,), (0,)), ((), ())), precision=lax.Precision.HIGHEST
    )
    inverse = 1.0 / per_bin
    for f in range(FRAMES):
        white[f, :NBIN, :] = (spectrum[f, :NBIN, :] * inverse).astype(BF16)
        white[f, NBIN:, :] = (spectrum[f, NBIN:, :] * inverse).astype(BF16)
    which = lax.broadcasted_iota(jnp.int32, (SOURCES, WIDTH), 0)
    channel = first[0] + lax.broadcasted_iota(jnp.int32, (SOURCES, WIDTH), 1)
    wanted = jnp.zeros((SOURCES, WIDTH), jnp.int32)
    for s in range(SOURCES):
        wanted = jnp.where(which == s, sources[s], wanted)
    onehot = jnp.where(wanted == channel, 1.0, 0.0).astype(BF16)
    for c in range(CHUNKS):
        rows = jnp.concatenate(chunk_rows(white, c), axis=0)
        found = lax.dot_general(
            onehot, rows, (((1,), (1,)), ((), ())), preferred_element_type=F32
        ).astype(BF16)
        picked[2 * c] = found[:, :WIDTH]
        picked[2 * c + 1] = found[:, WIDTH:]


SMEM = pl.BlockSpec(memory_space=pltpu.SMEM)
VMEM = pl.BlockSpec(memory_space=pltpu.VMEM)


def whiten(raw, taps, edges, sources, first):
    turns, tap_turns = turn_tables()
    return pl.pallas_call(
        whiten_kernel,
        out_shape=(
            jax.ShapeDtypeStruct((FRAMES, NFFT, WIDTH), BF16),
            jax.ShapeDtypeStruct((2 * CHUNKS, SOURCES, WIDTH), BF16),
        ),
        in_specs=[SMEM] + [pl.BlockSpec(memory_space=pl.ANY)] * 6,
        out_specs=(VMEM, VMEM),
        scratch_shapes=[
            pltpu.SMEM((TAPS,), F32),
            pltpu.SMEM((BANDS + 1,), jnp.int32),
            pltpu.SMEM((SOURCES,), jnp.int32),
            pltpu.VMEM((2, NBIN, SPAN_LANES), F32),
            pltpu.VMEM((NFFT, TAPS), F32),
            pltpu.VMEM((SAMPLES, WIDTH), BF16),
            pltpu.VMEM((3 * NFFT, SPAN_LANES), BF16),
            pltpu.VMEM((FRAMES, NFFT, WIDTH), F32),
            pltpu.SemaphoreType.DMA((6,)),
        ],
        name="whiten",
    )(first, taps, edges, sources, jnp.asarray(turns), jnp.asarray(tap_turns), raw)


def coherence_kernel(offsets, edges, own, near, far, out, ext, high, low):
    for f in range(FRAMES):
        ext[0, f] = own[f]
        ext[1, f] = near[f]
        ext[2, f] = far[f]
    lane = lax.broadcasted_iota(jnp.int32, (1, WIDTH), 1)
    step = 16

    def place(offset):
        first = offset // WIDTH
        turn = offset % WIDTH
        wrapped = jnp.broadcast_to(lane < turn, (step, WIDTH))
        return first, jnp.minimum(first + 1, 2), wrapped, (WIDTH - turn) % WIDTH

    def partner(where, f, start):
        first, second, wrapped, shift = where
        a = ext[first, f, start : start + step, :]
        b = ext[second, f, start : start + step, :]
        return pltpu.roll(jnp.where(wrapped, b, a), shift, 1).astype(F32)

    def pairs(i, _):
        places = [place(offsets[4 * i + n]) for n in range(4)]
        for k in range(0, NBIN, step):
            real = [jnp.zeros((step, WIDTH), F32) for _ in places]
            imag = [jnp.zeros((step, WIDTH), F32) for _ in places]
            for f in range(FRAMES):
                w_re = own[f, k : k + step, :].astype(F32)
                w_im = own[f, NBIN + k : NBIN + k + step, :].astype(F32)
                for n, where in enumerate(places):
                    p_re, p_im = partner(where, f, k), partner(where, f, NBIN + k)
                    real[n] += w_re * p_re + w_im * p_im
                    imag[n] += w_im * p_re - w_re * p_im
            for n in range(4):
                for part, cross in enumerate((real[n], imag[n])):
                    top = cross.astype(BF16)
                    high[4 * i + n, part, k : k + step, :] = top
                    low[4 * i + n, part, k : k + step, :] = (cross - top.astype(F32)).astype(BF16)
        return 0

    lax.fori_loop(0, OFFS // 4, pairs, 0)
    mask, bins = band_masks(edges)
    scale = 1.0 / jnp.sqrt(FRAMES * bins)
    bands = mask.astype(BF16)
    weights = jnp.concatenate([bands, bands], axis=1)
    for p in range(OFFS):
        real = jnp.concatenate([high[p, 0], low[p, 0]], axis=0)
        imag = jnp.concatenate([high[p, 1], low[p, 1]], axis=0)
        total = jnp.dot(
            weights, jnp.concatenate([real, imag], axis=1), preferred_element_type=F32
        )
        out[p, :BANDS, :] = total[:, :WIDTH] * scale
        out[p, BANDS:, :] = total[:, WIDTH:] * scale


def coherences(offsets, edges, own, near, far):
    return pl.pallas_call(
        coherence_kernel,
        out_shape=jax.ShapeDtypeStruct((OFFS, 2 * BANDS, WIDTH), F32),
        in_specs=[SMEM] * 2 + [VMEM] * 3,
        out_specs=VMEM,
        scratch_shapes=[
            pltpu.VMEM((3, FRAMES, NFFT, WIDTH), BF16),
            pltpu.VMEM((OFFS, 2, NBIN, WIDTH), BF16),
            pltpu.VMEM((OFFS, 2, NBIN, WIDTH), BF16),
        ],
        compiler_params=pltpu.CompilerParams(vmem_limit_bytes=VMEM_LIMIT),
        name="coherence",
    )(offsets, edges, own, near, far)


S_STEP = 8


def correlate_kernel(table, sources, white, out, left, high, low, held, sems):
    if True:
        row = lax.broadcasted_iota(jnp.int32, (CHUNK, NFFT), 0)
        column = lax.broadcasted_iota(jnp.int32, (CHUNK, NFFT), 1)
        diagonal = (column % CHUNK) == row
        for c in range(CHUNKS):
            values = jnp.concatenate([sources[2 * c], sources[2 * c + 1]], axis=1).astype(F32)
            for s in range(SOURCES):
                spread = jnp.broadcast_to(values[s : s + 1, :], (CHUNK, NFFT))
                left[s * CHUNK : (s + 1) * CHUNK, :] = jnp.where(diagonal, spread, 0.0).astype(BF16)
            rows = chunk_rows(white, c)
            turned = []
            for f in range(FRAMES):
                turned += [-rows[2 * f + 1], rows[2 * f]]
            right = jnp.concatenate(
                [jnp.concatenate(rows, axis=0), jnp.concatenate(turned, axis=0)], axis=1
            )
            cross = jnp.dot(left[...], right, preferred_element_type=F32)
            top = cross.astype(BF16)
            rest = (cross - top.astype(F32)).astype(BF16)
            for kept, value in ((high, top), (low, rest)):
                value = value.reshape(SOURCES, CHUNK, 2 * WIDTH)
                for part in range(2):
                    start = part * NBIN + c * CHUNK
                    kept[:, start : start + CHUNK, :] = value[:, :, part * WIDTH : (part + 1) * WIDTH]

    copies = []
    for g in range(SOURCES // S_STEP):
        for i in range(0, S_STEP, 2):
            s = g * S_STEP + i
            top = jnp.concatenate([high[s], high[s + 1]], axis=1)
            rest = jnp.concatenate([low[s], low[s + 1]], axis=1)
            both = jnp.dot(table[...], top, preferred_element_type=F32)
            lagged = both[:LAG_ROWS] + both[LAG_ROWS:]
            lagged += jnp.dot(table[:LAG_ROWS, :], rest, preferred_element_type=F32)
            held[g, :, i, :] = lagged[:LAGS, :WIDTH]
            held[g, :, i + 1, :] = lagged[:LAGS, WIDTH:]
        copies.append(
            pltpu.make_async_copy(
                held.at[g], out.at[:, pl.ds(g * S_STEP, S_STEP), :], sems.at[g]
            )
        )
        copies[-1].start()
    for copy in copies:
        copy.wait()


def correlations(sources, white):
    return pl.pallas_call(
        correlate_kernel,
        out_shape=jax.ShapeDtypeStruct((LAGS, SOURCES, WIDTH), F32),
        in_specs=[VMEM] * 3,
        out_specs=pl.BlockSpec(memory_space=pl.ANY),
        scratch_shapes=[
            pltpu.VMEM((SOURCES * CHUNK, NFFT), BF16),
            pltpu.VMEM((SOURCES, NFFT, WIDTH), BF16),
            pltpu.VMEM((SOURCES, NFFT, WIDTH), BF16),
            pltpu.VMEM((SOURCES // S_STEP, LAGS, S_STEP, WIDTH), F32),
            pltpu.SemaphoreType.DMA((SOURCES // S_STEP,)),
        ],
        compiler_params=pltpu.CompilerParams(vmem_limit_bytes=VMEM_LIMIT),
        name="correlate",
    )(jnp.asarray(lag_tables()), sources, white).transpose(1, 0, 2)


def from_behind(block, axis, distance):
    devices = range(lax.axis_size(axis))
    route = [((i - distance) % len(devices), i) for i in devices]
    return lax.ppermute(block, axis, route)


def sum_kernel(parts, out):
    total = jnp.sum(parts[...].astype(F32), axis=0).astype(BF16)
    out[...] = jnp.broadcast_to(total[None], out.shape)


def sum_copies(parts, count):
    return pl.pallas_call(
        sum_kernel,
        out_shape=jax.ShapeDtypeStruct((count,) + parts.shape[1:], BF16),
        in_specs=[VMEM],
        out_specs=VMEM,
        cost_estimate=pl.CostEstimate(flops=10_000, bytes_accessed=1 << 20, transcendentals=0),
        compiler_params=pltpu.CompilerParams(vmem_limit_bytes=VMEM_LIMIT),
        name="sum_copies",
    )(parts)


def spread_sources(picked, work):
    size = lax.axis_size("ch")
    runs = [list(range(g, g + RUN)) for g in range(0, size, RUN)]
    places = [list(range(g, size, RUN)) for g in range(RUN)]
    shape = picked.shape
    mine = picked.reshape(RUN, -1, WIDTH)
    mine = lax.all_to_all(mine, "ch", 0, 0, axis_index_groups=runs, tiled=True)
    copies = sum_copies(mine, size // RUN)
    mine = lax.all_to_all(copies, "ch", 0, 0, axis_index_groups=places, tiled=True)
    copies = sum_copies(mine, RUN)
    copies, done = lax.optimization_barrier((copies, work()))
    found = lax.all_to_all(copies, "ch", 0, 0, axis_index_groups=runs, tiled=True)
    return done, found.reshape(shape)


def per_device(raw, taps, offsets, sources, edges):
    first = jnp.full((1,), lax.axis_index("ch") * WIDTH, jnp.int32)
    white, picked = whiten(raw, taps, edges, sources, first)
    near = from_behind(white, "ch", -1)
    far = from_behind(white, "ch", -2)
    (near, far), found = spread_sources(picked, lambda: (near, far))
    coherence = coherences(offsets, edges, white, near, far)
    correlation = correlations(found, white)
    return (coherence, correlation)


def solution(mesh):
    in_specs = (P(None, "ch"), P(), P(), P(), P())
    out_specs = (P(None, None, "ch"), P(None, None, "ch"))
    return jax.shard_map(
        per_device, mesh=mesh, in_specs=in_specs, out_specs=out_specs, check_vma=False
    )
```

```python
import math

import jax
import jax.numpy as jnp
import numpy as np
from jax import lax
from jax.experimental import pallas as pl
from jax.experimental.pallas import tpu as pltpu
from jax.sharding import PartitionSpec as P

SAMPLES = 4096
TAPS = 16
NFFT = 256
FRAMES = 8
NBIN = 128
BANDS = 16
SOURCES = 32
OFFS = 16
MAXLAG = 64
LAGS = 129
LAG_ROWS = 144
WIDTH = 128
HALO = 16
SPAN = 2 * NFFT + HALO
SPAN_LANES = 640
CHUNK = 16
CHUNKS = NBIN // CHUNK
RUN = 16
VMEM_LIMIT = 48 * 1024 * 1024
F32 = jnp.float32
BF16 = jnp.bfloat16


def turn_tables():
    sample = np.arange(SPAN)[None, :] - HALO
    bins = np.arange(NBIN)[:, None]
    phase = bins * sample % (2 * NFFT) * (math.pi / NFFT)
    turns = np.stack([np.cos(phase), np.sin(phase)]).astype(np.float32)
    turns = np.pad(turns, ((0, 0), (0, 0), (0, SPAN_LANES - SPAN)))
    phase = bins * np.arange(TAPS)[None, :] % (2 * NFFT) * (math.pi / NFFT)
    return turns, np.concatenate([np.cos(phase), -np.sin(phase)], axis=0).astype(np.float32)


def lag_tables():
    lags = np.arange(LAGS) - MAXLAG
    phase = lags[:, None] * np.arange(NBIN)[None, :] % NFFT * (2.0 * math.pi / NFFT)
    table = np.concatenate([np.cos(phase), -np.sin(phase)], axis=1) / math.sqrt(FRAMES * NBIN)
    table = np.pad(table, ((0, LAG_ROWS - LAGS), (0, 0))).astype(np.float32)
    high = table.astype(BF16)
    low = (table - high.astype(np.float32)).astype(BF16)
    return np.concatenate([high, low], axis=0)


def chunk_rows(white, c):
    rows = []
    for f in range(FRAMES):
        for part in range(2):
            start = part * NBIN + c * CHUNK
            rows.append(white[f, start : start + CHUNK, :])
    return rows


def band_masks(edges):
    band = lax.broadcasted_iota(jnp.int32, (BANDS, NBIN), 0)
    bins = lax.broadcasted_iota(jnp.int32, (BANDS, NBIN), 1)
    lowest = jnp.zeros((BANDS, NBIN), jnp.int32)
    limit = jnp.zeros((BANDS, NBIN), jnp.int32)
    for b in range(BANDS):
        lowest = jnp.where(band == b, edges[b], lowest)
        limit = jnp.where(band == b, edges[b + 1], limit)
    mask = jnp.where((bins >= lowest) & (bins < limit), 1.0, 0.0).astype(F32)
    return mask, (limit - lowest).astype(F32)


def filtered_table(taps, turns, tap_turns, table):
    tap = lax.broadcasted_iota(jnp.int32, (TAPS, WIDTH), 0)
    lane = lax.broadcasted_iota(jnp.int32, (TAPS, WIDTH), 1)
    value = jnp.zeros((TAPS, WIDTH), F32)
    for j in range(TAPS):
        value = jnp.where(tap == j, taps[j], value)
    value = jnp.where((lane + tap) % 2 == 0, value, 0.0)
    early = jnp.where(lane + tap >= HALO, value, 0.0)
    late = jnp.where(lane + tap < HALO, value, 0.0)
    meets = jnp.concatenate([early, value, late], axis=1)
    response = jnp.dot(tap_turns[...], meets, precision=lax.Precision.HIGHEST)
    for block in range(SPAN_LANES // WIDTH):
        lanes = slice(block * WIDTH, (block + 1) * WIDTH)
        kind = 0 if block == 0 else 2 if block == SPAN_LANES // WIDTH - 1 else 1
        re = response[:NBIN, kind * WIDTH : (kind + 1) * WIDTH]
        im = response[NBIN:, kind * WIDTH : (kind + 1) * WIDTH]
        cos, sin = turns[0, :, lanes], turns[1, :, lanes]
        for half, rest in enumerate((cos * re + sin * im, cos * im - sin * re)):
            for part in range(3):
                piece = rest.astype(BF16)
                row = part * NFFT + half * NBIN
                table[row : row + NBIN, lanes] = piece
                rest = rest - piece.astype(F32)


def whiten_kernel(
    first, taps_hbm, edges_hbm, sources_hbm, turns_hbm, tap_turns_hbm, raw_hbm,
    white, picked,
    taps, edges, sources, turns, tap_turns, raw, table, spectrum, sems,
):
    loads = [
        pltpu.make_async_copy(src, dst, sems.at[i])
        for i, (src, dst) in enumerate(
            (
                (taps_hbm, taps),
                (tap_turns_hbm, tap_turns),
                (turns_hbm, turns),
                (raw_hbm, raw),
                (edges_hbm, edges),
                (sources_hbm, sources),
            )
        )
    ]
    for load in loads:
        load.start()
    for load in loads[:3]:
        load.wait()
    filtered_table(taps, turns, tap_turns, table)
    for load in loads[3:]:
        load.wait()
    squares = jnp.zeros((NFFT, WIDTH), F32)
    halo = [jnp.zeros((HALO, WIDTH), BF16)]
    halo += [raw[f * 2 * NFFT - HALO : f * 2 * NFFT, :] for f in range(1, FRAMES)]
    for f in range(0, FRAMES, 2):
        pair = [
            jnp.concatenate([halo[g], raw[g * 2 * NFFT : (g + 1) * 2 * NFFT, :]], axis=0)
            for g in (f, f + 1)
        ]
        parts = jnp.dot(
            table[:, :SPAN], jnp.concatenate(pair, axis=1), preferred_element_type=F32
        )
        both = parts[:NFFT] + parts[NFFT : 2 * NFFT] + parts[2 * NFFT :]
        for g in range(2):
            total = both[:, g * WIDTH : (g + 1) * WIDTH]
            spectrum[f + g] = total
            squares += total * total
    squares = squares[:NBIN] + squares[NBIN:]
    mask, bins = band_masks(edges)
    power = jnp.dot(mask, squares, precision=lax.Precision.HIGHEST) / (2.0 * FRAMES * bins)
    level = jnp.sqrt(power + 1e-06)
    per_bin = lax.dot_general(
        mask, level, (((0,), (0,)), ((), ())), precision=lax.Precision.HIGHEST
    )
    inverse = 1.0 / per_bin
    for f in range(FRAMES):
        white[f, :NBIN, :] = (spectrum[f, :NBIN, :] * inverse).astype(BF16)
        white[f, NBIN:, :] = (spectrum[f, NBIN:, :] * inverse).astype(BF16)
    which = lax.broadcasted_iota(jnp.int32, (SOURCES, WIDTH), 0)
    channel = first[0] + lax.broadcasted_iota(jnp.int32, (SOURCES, WIDTH), 1)
    wanted = jnp.zeros((SOURCES, WIDTH), jnp.int32)
    for s in range(SOURCES):
        wanted = jnp.where(which == s, sources[s], wanted)
    onehot = jnp.where(wanted == channel, 1.0, 0.0).astype(BF16)
    for c in range(CHUNKS):
        rows = jnp.concatenate(chunk_rows(white, c), axis=0)
        found = lax.dot_general(
            onehot, rows, (((1,), (1,)), ((), ())), preferred_element_type=F32
        ).astype(BF16)
        picked[2 * c] = found[:, :WIDTH]
        picked[2 * c + 1] = found[:, WIDTH:]


SMEM = pl.BlockSpec(memory_space=pltpu.SMEM)
VMEM = pl.BlockSpec(memory_space=pltpu.VMEM)


def whiten(raw, taps, edges, sources, first):
    turns, tap_turns = turn_tables()
    return pl.pallas_call(
        whiten_kernel,
        out_shape=(
            jax.ShapeDtypeStruct((FRAMES, NFFT, WIDTH), BF16),
            jax.ShapeDtypeStruct((2 * CHUNKS, SOURCES, WIDTH), BF16),
        ),
        in_specs=[SMEM] + [pl.BlockSpec(memory_space=pl.ANY)] * 6,
        out_specs=(VMEM, VMEM),
        scratch_shapes=[
            pltpu.SMEM((TAPS,), F32),
            pltpu.SMEM((BANDS + 1,), jnp.int32),
            pltpu.SMEM((SOURCES,), jnp.int32),
            pltpu.VMEM((2, NBIN, SPAN_LANES), F32),
            pltpu.VMEM((NFFT, TAPS), F32),
            pltpu.VMEM((SAMPLES, WIDTH), BF16),
            pltpu.VMEM((3 * NFFT, SPAN_LANES), BF16),
            pltpu.VMEM((FRAMES, NFFT, WIDTH), F32),
            pltpu.SemaphoreType.DMA((6,)),
        ],
        name="whiten",
    )(first, taps, edges, sources, jnp.asarray(turns), jnp.asarray(tap_turns), raw)


def coherence_kernel(odd, offsets, edges, own, other, arrived, swapped, out, ext, high, low):
    for f in range(FRAMES):
        ext[0, f] = own[f]
        ext[2, f] = swapped[f]

    @pl.when(odd[0] == 0)
    def _():
        ext[1] = other[...]

    @pl.when(odd[0] == 1)
    def _():
        ext[1] = arrived[...]

    lane = lax.broadcasted_iota(jnp.int32, (1, WIDTH), 1)
    step = 16

    def place(offset):
        first = offset // WIDTH
        turn = offset % WIDTH
        wrapped = jnp.broadcast_to(lane < turn, (step, WIDTH))
        return first, jnp.minimum(first + 1, 2), wrapped, (WIDTH - turn) % WIDTH

    def partner(where, f, start):
        first, second, wrapped, shift = where
        a = ext[first, f, start : start + step, :]
        b = ext[second, f, start : start + step, :]
        return pltpu.roll(jnp.where(wrapped, b, a), shift, 1).astype(F32)

    def pairs(i, _):
        places = [place(offsets[4 * i + n]) for n in range(4)]
        for k in range(0, NBIN, step):
            real = [jnp.zeros((step, WIDTH), F32) for _ in places]
            imag = [jnp.zeros((step, WIDTH), F32) for _ in places]
            for f in range(FRAMES):
                w_re = own[f, k : k + step, :].astype(F32)
                w_im = own[f, NBIN + k : NBIN + k + step, :].astype(F32)
                for n, where in enumerate(places):
                    p_re, p_im = partner(where, f, k), partner(where, f, NBIN + k)
                    real[n] += w_re * p_re + w_im * p_im
                    imag[n] += w_im * p_re - w_re * p_im
            for n in range(4):
                for part, cross in enumerate((real[n], imag[n])):
                    top = cross.astype(BF16)
                    high[4 * i + n, part, k : k + step, :] = top
                    low[4 * i + n, part, k : k + step, :] = (cross - top.astype(F32)).astype(BF16)
        return 0

    lax.fori_loop(0, OFFS // 4, pairs, 0)
    mask, bins = band_masks(edges)
    scale = 1.0 / jnp.sqrt(FRAMES * bins)
    bands = mask.astype(BF16)
    weights = jnp.concatenate([bands, bands], axis=1)
    for p in range(OFFS):
        real = jnp.concatenate([high[p, 0], low[p, 0]], axis=0)
        imag = jnp.concatenate([high[p, 1], low[p, 1]], axis=0)
        total = jnp.dot(
            weights, jnp.concatenate([real, imag], axis=1), preferred_element_type=F32
        )
        out[p, :BANDS, :] = total[:, :WIDTH] * scale
        out[p, BANDS:, :] = total[:, WIDTH:] * scale


def coherences(odd, offsets, edges, own, other, arrived, swapped):
    return pl.pallas_call(
        coherence_kernel,
        out_shape=jax.ShapeDtypeStruct((OFFS, 2 * BANDS, WIDTH), F32),
        in_specs=[SMEM] * 3 + [VMEM] * 4,
        out_specs=VMEM,
        scratch_shapes=[
            pltpu.VMEM((3, FRAMES, NFFT, WIDTH), BF16),
            pltpu.VMEM((OFFS, 2, NBIN, WIDTH), BF16),
            pltpu.VMEM((OFFS, 2, NBIN, WIDTH), BF16),
        ],
        compiler_params=pltpu.CompilerParams(vmem_limit_bytes=VMEM_LIMIT),
        name="coherence",
    )(odd, offsets, edges, own, other, arrived, swapped)


S_STEP = 8


def correlate_kernel(table, sources, white, out, left, high, low, held, sems):
    if True:
        row = lax.broadcasted_iota(jnp.int32, (CHUNK, NFFT), 0)
        column = lax.broadcasted_iota(jnp.int32, (CHUNK, NFFT), 1)
        diagonal = (column % CHUNK) == row
        for c in range(CHUNKS):
            values = jnp.concatenate([sources[2 * c], sources[2 * c + 1]], axis=1).astype(F32)
            for s in range(SOURCES):
                spread = jnp.broadcast_to(values[s : s + 1, :], (CHUNK, NFFT))
                left[s * CHUNK : (s + 1) * CHUNK, :] = jnp.where(diagonal, spread, 0.0).astype(BF16)
            rows = chunk_rows(white, c)
            turned = []
            for f in range(FRAMES):
                turned += [-rows[2 * f + 1], rows[2 * f]]
            right = jnp.concatenate(
                [jnp.concatenate(rows, axis=0), jnp.concatenate(turned, axis=0)], axis=1
            )
            cross = jnp.dot(left[...], right, preferred_element_type=F32)
            top = cross.astype(BF16)
            rest = (cross - top.astype(F32)).astype(BF16)
            for kept, value in ((high, top), (low, rest)):
                value = value.reshape(SOURCES, CHUNK, 2 * WIDTH)
                for part in range(2):
                    start = part * NBIN + c * CHUNK
                    kept[:, start : start + CHUNK, :] = value[:, :, part * WIDTH : (part + 1) * WIDTH]

    copies = []
    for g in range(SOURCES // S_STEP):
        for i in range(0, S_STEP, 2):
            s = g * S_STEP + i
            top = jnp.concatenate([high[s], high[s + 1]], axis=1)
            rest = jnp.concatenate([low[s], low[s + 1]], axis=1)
            both = jnp.dot(table[...], top, preferred_element_type=F32)
            lagged = both[:LAG_ROWS] + both[LAG_ROWS:]
            lagged += jnp.dot(table[:LAG_ROWS, :], rest, preferred_element_type=F32)
            held[g, :, i, :] = lagged[:LAGS, :WIDTH]
            held[g, :, i + 1, :] = lagged[:LAGS, WIDTH:]
        copies.append(
            pltpu.make_async_copy(
                held.at[g], out.at[:, pl.ds(g * S_STEP, S_STEP), :], sems.at[g]
            )
        )
        copies[-1].start()
    for copy in copies:
        copy.wait()


def correlations(sources, white):
    return pl.pallas_call(
        correlate_kernel,
        out_shape=jax.ShapeDtypeStruct((LAGS, SOURCES, WIDTH), F32),
        in_specs=[VMEM] * 3,
        out_specs=pl.BlockSpec(memory_space=pl.ANY),
        scratch_shapes=[
            pltpu.VMEM((SOURCES * CHUNK, NFFT), BF16),
            pltpu.VMEM((SOURCES, NFFT, WIDTH), BF16),
            pltpu.VMEM((SOURCES, NFFT, WIDTH), BF16),
            pltpu.VMEM((SOURCES // S_STEP, LAGS, S_STEP, WIDTH), F32),
            pltpu.SemaphoreType.DMA((SOURCES // S_STEP,)),
        ],
        compiler_params=pltpu.CompilerParams(vmem_limit_bytes=VMEM_LIMIT),
        name="correlate",
    )(jnp.asarray(lag_tables()), sources, white).transpose(1, 0, 2)


def from_next_chip(block):
    size = lax.axis_size("ch")
    route = [((i + 3 if i % 2 == 0 else i + 1) % size, i) for i in range(size)]
    return lax.ppermute(block, "ch", route)


def swap_in_chip(block):
    return lax.ppermute(block, "ch", [(i ^ 1, i) for i in range(lax.axis_size("ch"))])


def sum_kernel(parts, out):
    total = jnp.sum(parts[...].astype(F32), axis=0).astype(BF16)
    out[...] = jnp.broadcast_to(total[None], out.shape)


def sum_copies(parts, count):
    return pl.pallas_call(
        sum_kernel,
        out_shape=jax.ShapeDtypeStruct((count,) + parts.shape[1:], BF16),
        in_specs=[VMEM],
        out_specs=VMEM,
        cost_estimate=pl.CostEstimate(flops=10_000, bytes_accessed=1 << 20, transcendentals=0),
        compiler_params=pltpu.CompilerParams(vmem_limit_bytes=VMEM_LIMIT),
        name="sum_copies",
    )(parts)


def spread_sources(picked, work):
    size = lax.axis_size("ch")
    runs = [list(range(g, g + RUN)) for g in range(0, size, RUN)]
    places = [list(range(g, size, RUN)) for g in range(RUN)]
    shape = picked.shape
    mine = picked.reshape(RUN, -1, WIDTH)
    mine = lax.all_to_all(mine, "ch", 0, 0, axis_index_groups=runs, tiled=True)
    copies = sum_copies(mine, size // RUN)
    mine = lax.all_to_all(copies, "ch", 0, 0, axis_index_groups=places, tiled=True)
    copies = sum_copies(mine, RUN)
    copies, done = lax.optimization_barrier((copies, work()))
    found = lax.all_to_all(copies, "ch", 0, 0, axis_index_groups=runs, tiled=True)
    return done, found.reshape(shape)


def per_device(raw, taps, offsets, sources, edges):
    first = jnp.full((1,), lax.axis_index("ch") * WIDTH, jnp.int32)
    white, picked = whiten(raw, taps, edges, sources, first)
    odd = jnp.full((1,), lax.axis_index("ch") % 2, jnp.int32)
    arrived = from_next_chip(white)
    other = swap_in_chip(white)
    held, found = spread_sources(picked, lambda: (other, arrived))
    other, arrived = held
    coherence = coherences(odd, offsets, edges, white, other, arrived, swap_in_chip(arrived))
    coherence, found = lax.optimization_barrier((coherence, found))
    correlation = correlations(found, white)
    return (coherence, correlation)


def solution(mesh):
    in_specs = (P(None, "ch"), P(), P(), P(), P())
    out_specs = (P(None, None, "ch"), P(None, None, "ch"))
    return jax.shard_map(
        per_device, mesh=mesh, in_specs=in_specs, out_specs=out_specs, check_vma=False
    )
```

```python
import math

import jax
import jax.numpy as jnp
import numpy as np
from jax import lax
from jax.experimental import pallas as pl
from jax.experimental.pallas import tpu as pltpu
from jax.sharding import PartitionSpec as P

SAMPLES = 4096
TAPS = 16
NFFT = 256
FRAMES = 8
NBIN = 128
BANDS = 16
SOURCES = 32
OFFS = 16
MAXLAG = 64
LAGS = 129
LAG_ROWS = 144
WIDTH = 128
HALO = 16
SPAN = 2 * NFFT + HALO
SPAN_LANES = 640
CHUNK = 16
CHUNKS = NBIN // CHUNK
RUN = 16
VMEM_LIMIT = 48 * 1024 * 1024
F32 = jnp.float32
BF16 = jnp.bfloat16


def turn_tables():
    sample = np.arange(SPAN)[None, :] - HALO
    bins = np.arange(NBIN)[:, None]
    phase = bins * sample % (2 * NFFT) * (math.pi / NFFT)
    turns = np.stack([np.cos(phase), np.sin(phase)]).astype(np.float32)
    turns = np.pad(turns, ((0, 0), (0, 0), (0, SPAN_LANES - SPAN)))
    phase = bins * np.arange(TAPS)[None, :] % (2 * NFFT) * (math.pi / NFFT)
    return turns, np.concatenate([np.cos(phase), -np.sin(phase)], axis=0).astype(np.float32)


def lag_tables():
    lags = np.arange(LAGS) - MAXLAG
    phase = lags[:, None] * np.arange(NBIN)[None, :] % NFFT * (2.0 * math.pi / NFFT)
    table = np.concatenate([np.cos(phase), -np.sin(phase)], axis=1) / math.sqrt(FRAMES * NBIN)
    table = np.pad(table, ((0, LAG_ROWS - LAGS), (0, 0))).astype(np.float32)
    high = table.astype(BF16)
    low = (table - high.astype(np.float32)).astype(BF16)
    return np.concatenate([high, low], axis=0)


def chunk_rows(white, c):
    rows = []
    for f in range(FRAMES):
        for part in range(2):
            start = part * NBIN + c * CHUNK
            rows.append(white[f, start : start + CHUNK, :])
    return rows


def band_masks(edges):
    band = lax.broadcasted_iota(jnp.int32, (BANDS, NBIN), 0)
    bins = lax.broadcasted_iota(jnp.int32, (BANDS, NBIN), 1)
    lowest = jnp.zeros((BANDS, NBIN), jnp.int32)
    limit = jnp.zeros((BANDS, NBIN), jnp.int32)
    for b in range(BANDS):
        lowest = jnp.where(band == b, edges[b], lowest)
        limit = jnp.where(band == b, edges[b + 1], limit)
    mask = jnp.where((bins >= lowest) & (bins < limit), 1.0, 0.0).astype(F32)
    return mask, (limit - lowest).astype(F32)


def filtered_table(taps, turns, tap_turns, table):
    tap = lax.broadcasted_iota(jnp.int32, (TAPS, WIDTH), 0)
    lane = lax.broadcasted_iota(jnp.int32, (TAPS, WIDTH), 1)
    value = jnp.zeros((TAPS, WIDTH), F32)
    for j in range(TAPS):
        value = jnp.where(tap == j, taps[j], value)
    value = jnp.where((lane + tap) % 2 == 0, value, 0.0)
    early = jnp.where(lane + tap >= HALO, value, 0.0)
    late = jnp.where(lane + tap < HALO, value, 0.0)
    meets = jnp.concatenate([early, value, late], axis=1)
    response = jnp.dot(tap_turns[...], meets, precision=lax.Precision.HIGHEST)
    for block in range(SPAN_LANES // WIDTH):
        lanes = slice(block * WIDTH, (block + 1) * WIDTH)
        kind = 0 if block == 0 else 2 if block == SPAN_LANES // WIDTH - 1 else 1
        re = response[:NBIN, kind * WIDTH : (kind + 1) * WIDTH]
        im = response[NBIN:, kind * WIDTH : (kind + 1) * WIDTH]
        cos, sin = turns[0, :, lanes], turns[1, :, lanes]
        for half, rest in enumerate((cos * re + sin * im, cos * im - sin * re)):
            for part in range(3):
                piece = rest.astype(BF16)
                row = part * NFFT + half * NBIN
                table[row : row + NBIN, lanes] = piece
                rest = rest - piece.astype(F32)


def whiten_kernel(
    first, taps_hbm, edges_hbm, sources_hbm, turns_hbm, tap_turns_hbm, raw_hbm,
    white, picked,
    taps, edges, sources, turns, tap_turns, raw, table, spectrum, sems,
):
    loads = [
        pltpu.make_async_copy(src, dst, sems.at[i])
        for i, (src, dst) in enumerate(
            (
                (taps_hbm, taps),
                (tap_turns_hbm, tap_turns),
                (turns_hbm, turns),
                (raw_hbm, raw),
                (edges_hbm, edges),
                (sources_hbm, sources),
            )
        )
    ]
    for load in loads:
        load.start()
    for load in loads[:3]:
        load.wait()
    filtered_table(taps, turns, tap_turns, table)
    for load in loads[3:]:
        load.wait()
    squares = jnp.zeros((NFFT, WIDTH), F32)
    halo = [jnp.zeros((HALO, WIDTH), BF16)]
    halo += [raw[f * 2 * NFFT - HALO : f * 2 * NFFT, :] for f in range(1, FRAMES)]
    for f in range(0, FRAMES, 2):
        pair = [
            jnp.concatenate([halo[g], raw[g * 2 * NFFT : (g + 1) * 2 * NFFT, :]], axis=0)
            for g in (f, f + 1)
        ]
        parts = jnp.dot(
            table[:, :SPAN], jnp.concatenate(pair, axis=1), preferred_element_type=F32
        )
        both = parts[:NFFT] + parts[NFFT : 2 * NFFT] + parts[2 * NFFT :]
        for g in range(2):
            total = both[:, g * WIDTH : (g + 1) * WIDTH]
            spectrum[f + g] = total
            squares += total * total
    squares = squares[:NBIN] + squares[NBIN:]
    mask, bins = band_masks(edges)
    power = jnp.dot(mask, squares, precision=lax.Precision.HIGHEST) / (2.0 * FRAMES * bins)
    level = jnp.sqrt(power + 1e-06)
    per_bin = lax.dot_general(
        mask, level, (((0,), (0,)), ((), ())), precision=lax.Precision.HIGHEST
    )
    inverse = 1.0 / per_bin
    for f in range(FRAMES):
        white[f, :NBIN, :] = (spectrum[f, :NBIN, :] * inverse).astype(BF16)
        white[f, NBIN:, :] = (spectrum[f, NBIN:, :] * inverse).astype(BF16)
    which = lax.broadcasted_iota(jnp.int32, (SOURCES, WIDTH), 0)
    channel = first[0] + lax.broadcasted_iota(jnp.int32, (SOURCES, WIDTH), 1)
    wanted = jnp.zeros((SOURCES, WIDTH), jnp.int32)
    for s in range(SOURCES):
        wanted = jnp.where(which == s, sources[s], wanted)
    onehot = jnp.where(wanted == channel, 1.0, 0.0).astype(BF16)
    for c in range(CHUNKS):
        rows = jnp.concatenate(chunk_rows(white, c), axis=0)
        found = lax.dot_general(
            onehot, rows, (((1,), (1,)), ((), ())), preferred_element_type=F32
        ).astype(BF16)
        picked[2 * c] = found[:, :WIDTH]
        picked[2 * c + 1] = found[:, WIDTH:]


SMEM = pl.BlockSpec(memory_space=pltpu.SMEM)
VMEM = pl.BlockSpec(memory_space=pltpu.VMEM)


def whiten(raw, taps, edges, sources, first):
    turns, tap_turns = turn_tables()
    return pl.pallas_call(
        whiten_kernel,
        out_shape=(
            jax.ShapeDtypeStruct((FRAMES, NFFT, WIDTH), BF16),
            jax.ShapeDtypeStruct((2 * CHUNKS, SOURCES, WIDTH), BF16),
        ),
        in_specs=[SMEM] + [pl.BlockSpec(memory_space=pl.ANY)] * 6,
        out_specs=(VMEM, VMEM),
        scratch_shapes=[
            pltpu.SMEM((TAPS,), F32),
            pltpu.SMEM((BANDS + 1,), jnp.int32),
            pltpu.SMEM((SOURCES,), jnp.int32),
            pltpu.VMEM((2, NBIN, SPAN_LANES), F32),
            pltpu.VMEM((NFFT, TAPS), F32),
            pltpu.VMEM((SAMPLES, WIDTH), BF16),
            pltpu.VMEM((3 * NFFT, SPAN_LANES), BF16),
            pltpu.VMEM((FRAMES, NFFT, WIDTH), F32),
            pltpu.SemaphoreType.DMA((6,)),
        ],
        name="whiten",
    )(first, taps, edges, sources, jnp.asarray(turns), jnp.asarray(tap_turns), raw)


def coherence_kernel(odd, offsets, edges, own, arrived, sibling, out, ext, high, low):
    for f in range(FRAMES):
        ext[0, f] = own[f]
        ext[2, f] = sibling[1, f]

    @pl.when(odd[0] == 0)
    def _():
        ext[1] = sibling[0]

    @pl.when(odd[0] == 1)
    def _():
        ext[1] = arrived[...]

    lane = lax.broadcasted_iota(jnp.int32, (1, WIDTH), 1)
    step = 16

    def place(offset):
        first = offset // WIDTH
        turn = offset % WIDTH
        wrapped = jnp.broadcast_to(lane < turn, (step, WIDTH))
        return first, jnp.minimum(first + 1, 2), wrapped, (WIDTH - turn) % WIDTH

    def partner(where, f, start):
        first, second, wrapped, shift = where
        a = ext[first, f, start : start + step, :]
        b = ext[second, f, start : start + step, :]
        return pltpu.roll(jnp.where(wrapped, b, a), shift, 1).astype(F32)

    def pairs(i, _):
        places = [place(offsets[4 * i + n]) for n in range(4)]
        for k in range(0, NBIN, step):
            real = [jnp.zeros((step, WIDTH), F32) for _ in places]
            imag = [jnp.zeros((step, WIDTH), F32) for _ in places]
            for f in range(FRAMES):
                w_re = own[f, k : k + step, :].astype(F32)
                w_im = own[f, NBIN + k : NBIN + k + step, :].astype(F32)
                for n, where in enumerate(places):
                    p_re, p_im = partner(where, f, k), partner(where, f, NBIN + k)
                    real[n] += w_re * p_re + w_im * p_im
                    imag[n] += w_im * p_re - w_re * p_im
            for n in range(4):
                for part, cross in enumerate((real[n], imag[n])):
                    top = cross.astype(BF16)
                    high[4 * i + n, part, k : k + step, :] = top
                    low[4 * i + n, part, k : k + step, :] = (cross - top.astype(F32)).astype(BF16)
        return 0

    lax.fori_loop(0, OFFS // 4, pairs, 0)
    mask, bins = band_masks(edges)
    scale = 1.0 / jnp.sqrt(FRAMES * bins)
    bands = mask.astype(BF16)
    weights = jnp.concatenate([bands, bands], axis=1)
    for p in range(OFFS):
        real = jnp.concatenate([high[p, 0], low[p, 0]], axis=0)
        imag = jnp.concatenate([high[p, 1], low[p, 1]], axis=0)
        total = jnp.dot(
            weights, jnp.concatenate([real, imag], axis=1), preferred_element_type=F32
        )
        out[p, :BANDS, :] = total[:, :WIDTH] * scale
        out[p, BANDS:, :] = total[:, WIDTH:] * scale


def coherences(odd, offsets, edges, own, arrived, sibling):
    return pl.pallas_call(
        coherence_kernel,
        out_shape=jax.ShapeDtypeStruct((OFFS, 2 * BANDS, WIDTH), F32),
        in_specs=[SMEM] * 3 + [VMEM] * 3,
        out_specs=VMEM,
        scratch_shapes=[
            pltpu.VMEM((3, FRAMES, NFFT, WIDTH), BF16),
            pltpu.VMEM((OFFS, 2, NBIN, WIDTH), BF16),
            pltpu.VMEM((OFFS, 2, NBIN, WIDTH), BF16),
        ],
        compiler_params=pltpu.CompilerParams(vmem_limit_bytes=VMEM_LIMIT),
        name="coherence",
    )(odd, offsets, edges, own, arrived, sibling)


S_STEP = 8


def correlate_kernel(table, sources, white, out, left, high, low, held, sems):
    if True:
        row = lax.broadcasted_iota(jnp.int32, (CHUNK, NFFT), 0)
        column = lax.broadcasted_iota(jnp.int32, (CHUNK, NFFT), 1)
        diagonal = (column % CHUNK) == row
        for c in range(CHUNKS):
            values = jnp.concatenate([sources[2 * c], sources[2 * c + 1]], axis=1).astype(F32)
            for s in range(SOURCES):
                spread = jnp.broadcast_to(values[s : s + 1, :], (CHUNK, NFFT))
                left[s * CHUNK : (s + 1) * CHUNK, :] = jnp.where(diagonal, spread, 0.0).astype(BF16)
            rows = chunk_rows(white, c)
            turned = []
            for f in range(FRAMES):
                turned += [-rows[2 * f + 1], rows[2 * f]]
            right = jnp.concatenate(
                [jnp.concatenate(rows, axis=0), jnp.concatenate(turned, axis=0)], axis=1
            )
            cross = jnp.dot(left[...], right, preferred_element_type=F32)
            top = cross.astype(BF16)
            rest = (cross - top.astype(F32)).astype(BF16)
            for kept, value in ((high, top), (low, rest)):
                value = value.reshape(SOURCES, CHUNK, 2 * WIDTH)
                for part in range(2):
                    start = part * NBIN + c * CHUNK
                    kept[:, start : start + CHUNK, :] = value[:, :, part * WIDTH : (part + 1) * WIDTH]

    copies = []
    for g in range(SOURCES // S_STEP):
        for i in range(0, S_STEP, 2):
            s = g * S_STEP + i
            top = jnp.concatenate([high[s], high[s + 1]], axis=1)
            rest = jnp.concatenate([low[s], low[s + 1]], axis=1)
            both = jnp.dot(table[...], top, preferred_element_type=F32)
            lagged = both[:LAG_ROWS] + both[LAG_ROWS:]
            lagged += jnp.dot(table[:LAG_ROWS, :], rest, preferred_element_type=F32)
            held[g, :, i, :] = lagged[:LAGS, :WIDTH]
            held[g, :, i + 1, :] = lagged[:LAGS, WIDTH:]
        copies.append(
            pltpu.make_async_copy(
                held.at[g], out.at[:, pl.ds(g * S_STEP, S_STEP), :], sems.at[g]
            )
        )
        copies[-1].start()
    for copy in copies:
        copy.wait()


def correlations(sources, white):
    return pl.pallas_call(
        correlate_kernel,
        out_shape=jax.ShapeDtypeStruct((LAGS, SOURCES, WIDTH), F32),
        in_specs=[VMEM] * 3,
        out_specs=pl.BlockSpec(memory_space=pl.ANY),
        scratch_shapes=[
            pltpu.VMEM((SOURCES * CHUNK, NFFT), BF16),
            pltpu.VMEM((SOURCES, NFFT, WIDTH), BF16),
            pltpu.VMEM((SOURCES, NFFT, WIDTH), BF16),
            pltpu.VMEM((SOURCES // S_STEP, LAGS, S_STEP, WIDTH), F32),
            pltpu.SemaphoreType.DMA((SOURCES // S_STEP,)),
        ],
        compiler_params=pltpu.CompilerParams(vmem_limit_bytes=VMEM_LIMIT),
        name="correlate",
    )(jnp.asarray(lag_tables()), sources, white).transpose(1, 0, 2)


def from_next_chip(block):
    size = lax.axis_size("ch")
    route = [((i + 3 if i % 2 == 0 else i + 1) % size, i) for i in range(size)]
    return lax.ppermute(block, "ch", route)


def swap_in_chip(block):
    return lax.ppermute(block, "ch", [(i ^ 1, i) for i in range(lax.axis_size("ch"))])


def sum_kernel(parts, out):
    total = jnp.sum(parts[...].astype(F32), axis=0).astype(BF16)
    out[...] = jnp.broadcast_to(total[None], out.shape)


def sum_copies(parts, count):
    return pl.pallas_call(
        sum_kernel,
        out_shape=jax.ShapeDtypeStruct((count,) + parts.shape[1:], BF16),
        in_specs=[VMEM],
        out_specs=VMEM,
        cost_estimate=pl.CostEstimate(flops=10_000, bytes_accessed=1 << 20, transcendentals=0),
        compiler_params=pltpu.CompilerParams(vmem_limit_bytes=VMEM_LIMIT),
        name="sum_copies",
    )(parts)


def spread_sources(picked, work):
    size = lax.axis_size("ch")
    runs = [list(range(g, g + RUN)) for g in range(0, size, RUN)]
    places = [list(range(g, size, RUN)) for g in range(RUN)]
    shape = picked.shape
    mine = picked.reshape(RUN, -1, WIDTH)
    mine = lax.all_to_all(mine, "ch", 0, 0, axis_index_groups=runs, tiled=True)
    copies = sum_copies(mine, size // RUN)
    mine = lax.all_to_all(copies, "ch", 0, 0, axis_index_groups=places, tiled=True)
    copies = sum_copies(mine, RUN)
    copies, done = lax.optimization_barrier((copies, work()))
    found = lax.all_to_all(copies, "ch", 0, 0, axis_index_groups=runs, tiled=True)
    return done, found.reshape(shape)


def per_device(raw, taps, offsets, sources, edges):
    first = jnp.full((1,), lax.axis_index("ch") * WIDTH, jnp.int32)
    white, picked = whiten(raw, taps, edges, sources, first)
    odd = jnp.full((1,), lax.axis_index("ch") % 2, jnp.int32)
    landing = from_next_chip(white)
    arrived, found = spread_sources(picked, lambda: landing)
    sibling = swap_in_chip(jnp.stack([white, arrived]))
    coherence = coherences(odd, offsets, edges, white, arrived, sibling)
    coherence, found = lax.optimization_barrier((coherence, found))
    correlation = correlations(found, white)
    return (coherence, correlation)


def solution(mesh):
    in_specs = (P(None, "ch"), P(), P(), P(), P())
    out_specs = (P(None, None, "ch"), P(None, None, "ch"))
    return jax.shard_map(
        per_device, mesh=mesh, in_specs=in_specs, out_specs=out_specs, check_vma=False
    )
```
